256 devices in a mesh: blk: 32 (over z, y), zero: 8 (over x, core).
Axes of the slice: x: 4, y: 4, z: 8, core: 2. Of those that a mesh axis runs over, the one named last changes fastest.
Arguments:
- grads: bfloat16 [16, 512, 6144], P('zero', 'blk'), may hold values from -4200 to 4200
- owners: int32 [8, 24, 1], P('zero'), may hold values from 0 to 31; in each aligned block of 24 rows (0 to 23, 24 to 47, ..., all dimensions but the last counted through in order) at most 2 rows name the same one
- left_stats: float32 [8, 24, 512, 512], P('zero', None, 'blk'), may hold values from -1.5 to 50, as said below
- right_stats: float32 [8, 24, 512, 512], P('zero', None, 'blk'), may hold values from -1.5 to 50, as said below
- second_moment: float32 [16, 512, 6144], P('zero', 'blk'), may hold values from 0.01 to 0.2
- roots: bfloat16 [8, 2, 64, 512, 512], P('zero', None, 'blk'), may hold values from -0.02 to 0.45, as said below
Outputs:
- update: bfloat16 [16, 512, 6144], P('zero', 'blk')
- new_second: float32 [16, 512, 6144], P('zero', 'blk')
- new_left: float32 [8, 24, 512, 512], P('zero', None, 'blk')
- new_right: float32 [8, 24, 512, 512], P('zero', None, 'blk')
- new_roots: bfloat16 [8, 2, 64, 512, 512], P('zero', None, 'blk')
The draws below stay inside these ranges and needn't reach their ends.
Inputs may be any that keep to these rules, and one draw needn't show every extreme that they name: `owners`: within the 24 blocks of one index of zero no owner is named by more than 2 blocks, and in some index of zero an owner is named by exactly 2. `left_stats`: each block is symmetric. `right_stats`: each block is symmetric. `roots`: each block is symmetric.
All inputs are finite; a program needn't handle non-finite values.
Results may differ from the reference program's by a relative error of at most 0.0068.
Values may be sent and summed in bfloat16 or wider, within the bound.
No kernel may reach another device: no remote copies, remote signals or barrier semaphores. Data moves between devices by JAX's collectives and lax.ppermute only.
A program may use at most 64 MiB of HBM per device.

```python
import math
import jax
import jax.numpy as jnp
import numpy as np
from jax import lax

D = 6144
B = 512
RB_DEV = 2
CB = 12
NBG = 24
RB = 16
SLOTS = 2
N_BLK = 32
N_ZERO = 8


def symmetric_block(noise, diagonal, size):
    mirrored = (noise + jnp.swapaxes(noise, -1, -2)) * 0.70710678
    identity = jnp.eye(size, dtype=jnp.float32)
    return mirrored * (1.0 - identity) + diagonal[..., None] * identity


def log_spread(key, shape, lower, upper):
    return jnp.exp(jax.random.uniform(key, shape, jnp.float32, math.log(lower), math.log(upper)))


def draw_grads(key, part):
    key = jax.random.fold_in(key, 11)
    first, second, third = jax.random.split(key, 3)
    shape = (RB, B, D)
    noise = jnp.clip(jax.random.normal(first, shape, jnp.float32), -4.0, 4.0)
    upper = 10.0
    rows = log_spread(second, (RB, B, 1), 1.0, upper)
    columns = log_spread(third, (1, 1, D), 1.0, upper)
    within = jnp.exp(math.log(3.0) * jnp.arange(B, dtype=jnp.float32) / B).reshape(1, B, 1)
    across = jnp.exp(math.log(3.0) * jnp.arange(RB, dtype=jnp.float32) / RB).reshape(RB, 1, 1)
    return (noise * rows * columns * within * across).astype(jnp.bfloat16)


def draw_left_stats(key, part):
    key = jax.random.fold_in(key, 21)
    first, second = jax.random.split(key)
    shape = (N_ZERO, NBG, B, B)
    noise = 0.26 * jnp.clip(jax.random.normal(first, shape, jnp.float32), -4.0, 4.0)
    diagonal = log_spread(second, (N_ZERO, NBG, B), 12.0, 50.0)
    return symmetric_block(noise, diagonal, B)


def draw_right_stats(key, part):
    key = jax.random.fold_in(key, 31)
    first, second = jax.random.split(key)
    shape = (N_ZERO, NBG, B, B)
    noise = 0.26 * jnp.clip(jax.random.normal(first, shape, jnp.float32), -4.0, 4.0)
    diagonal = log_spread(second, (N_ZERO, NBG, B), 12.0, 50.0)
    return symmetric_block(noise, diagonal, B)


def draw_roots(key, part):
    key = jax.random.fold_in(key, 41)
    first, second = jax.random.split(key)
    shape = (N_ZERO, 2, N_BLK * SLOTS, B, B)
    noise = 0.0033 * jnp.clip(jax.random.normal(first, shape, jnp.float32), -4.0, 4.0)
    diagonal = log_spread(second, shape[:4], 0.28, 0.44)
    return symmetric_block(noise, diagonal, B).astype(jnp.bfloat16)


def block_levels(key, dims, pieces, least, largest):
    level = 1.0
    for position, shards_of in pieces:
        heights = jax.random.uniform(jax.random.fold_in(jax.random.fold_in(key, 6), position), (shards_of,), jnp.float32, least / len(pieces), largest / len(pieces))
        level = level * jnp.repeat(jnp.exp(heights), dims[position] // shards_of).reshape((-1,) + (1,) * (len(dims) - 1 - position))
    return level


def routed_block(own_key, own, number, rows, amount, top, limit, lean):
    order = jax.random.permutation(own_key, amount)
    packed, usual = load_shares(amount, rows * top, limit, lean, True), load_shares(amount, rows * top, limit, lean, False)
    places = jnp.arange(amount)

    def named(lengths, turn):
        used = int((lengths > 0).sum())
        fixed = max(1, used // 4)
        shifted = fixed + (places - fixed + turn * (used - fixed)) % max(1, amount - fixed)
        return jnp.zeros((amount,), jnp.int32).at[order[jnp.where(places < fixed, places, shifted)]].set(jnp.asarray(lengths, jnp.int32))

    lengths = jnp.where(number % 4 == 0, named(packed, number // 4), named(usual, number - number // 4 - 1))
    mixed = jax.random.permutation(jax.random.fold_in(own, 3), amount)
    giver, taker = mixed[0:amount // 2 * 2:2], mixed[1:amount // 2 * 2:2]
    room = jnp.minimum(lengths[giver] - 1, limit - lengths[taker]) // 2
    room = jnp.where((giver == order[0]) | (taker == order[0]) | (lengths[taker] == 0), 0, jnp.maximum(room, 0))
    shifted = jax.random.randint(jax.random.fold_in(own, 4), (amount // 2,), 0, 1 << 20) % (room + 1)
    lengths = lengths.at[giver].add(-shifted).at[taker].add(shifted)
    members = jnp.searchsorted(jnp.cumsum(lengths), jnp.arange(rows * top), side="right").astype(jnp.int32)
    table = members.reshape(top, rows).T
    table = table[jax.random.permutation(jax.random.fold_in(own, 1), rows)]
    turn = jax.random.randint(jax.random.fold_in(own, 2), (rows, 1), 0, top)
    return jnp.take_along_axis(table, (jnp.arange(top)[None, :] + turn) % top, axis=1)


def load_shares(amount, total, limit, lean, full):
    portions = [(1 << 20) // math.isqrt(grade ** lean) + 1 for grade in range(1, amount + 1)]
    largest = limit if full else min(limit, max(-(-total // amount), total * portions[0] // sum(portions)))
    least = 1 if total - largest >= amount - 1 else 0
    holding, surplus = [largest] + [least] * (amount - 1), total - largest - least * (amount - 1)
    while surplus > 0:
        free = [i for i in range(1, amount) if holding[i] < largest] or [i for i in range(1, amount) if holding[i] < limit]
        whole, left = sum([portions[i] for i in free]), surplus
        for i in free:
            more = min(limit - holding[i], max(1, left * portions[i] // whole), surplus)
            holding[i] = holding[i] + more
            surplus = surplus - more
    return np.array(holding)


def setup_inputs(seed: int = 0) -> dict:
    streams_of = jax.random.split(jax.random.key(seed), 7)
    grads = draw_grads(jax.random.fold_in(streams_of[6], 71), 0)
    owners_keys = jax.random.split(jax.random.fold_in(streams_of[1], 1), N_ZERO * NBG // NBG)
    owners_turns = jax.random.permutation(jax.random.fold_in(streams_of[1], 3), N_ZERO * NBG // NBG)
    owners = jax.vmap(lambda own, number: routed_block(jax.random.fold_in(streams_of[1], 2), own, number, NBG, N_BLK, 1, SLOTS, 2))(owners_keys, owners_turns).reshape((N_ZERO, NBG, 1))
    left_stats = draw_left_stats(jax.random.fold_in(streams_of[6], 71), 0)
    right_stats = draw_right_stats(jax.random.fold_in(streams_of[6], 71), 0)
    second_moment = jnp.clip(jnp.exp(math.log(0.2) - 2.9957323 * jax.random.uniform(streams_of[4], (RB, B, D), jnp.float32) ** block_levels(streams_of[4], (RB, B, D), ((0, 8), (1, 32)), -0.2, 0.2)), 0.01, 0.2)
    roots = draw_roots(jax.random.fold_in(streams_of[6], 71), 0)
    return dict(grads=grads, owners=owners, left_stats=left_stats, right_stats=right_stats, second_moment=second_moment, roots=roots)


BETA = 0.95

def full_dot(former, latter):
    return jnp.dot(former, latter, precision=lax.Precision.HIGHEST, preferred_element_type=jnp.float32)

def inverse_root(previous, statistic):
    seed_wide = previous.astype(jnp.float32)
    seed_square = full_dot(seed_wide, seed_wide)
    seed_fourth = full_dot(seed_square, seed_square)
    product = full_dot(seed_fourth, statistic)
    identity = jnp.eye(statistic.shape[0], dtype=jnp.float32)
    newton_step = (5.0 * identity - product) * 0.25
    return full_dot(seed_wide, newton_step).astype(jnp.bfloat16)

def reference(grads, owners, left_stats, right_stats, second_moment, roots):
    widened = grads.astype(jnp.float32)
    grand_total = jnp.sum(widened * widened)
    clip_scale = jnp.minimum(1.0, math.sqrt(RB * B * D) / (jnp.sqrt(grand_total) + 1e-06))
    clipped = widened * clip_scale
    new_second = 0.95 * second_moment + 0.05 * clipped * clipped
    adam_step = clipped / (jnp.sqrt(new_second) + 1e-08)
    adam_sq = lax.optimization_barrier(jnp.sum((adam_step * adam_step).reshape(N_ZERO, RB_DEV, B, CB, B), axis=(2, 4))).reshape(N_ZERO * NBG)
    blocks = grads.reshape(N_ZERO, RB_DEV, B, CB, B).transpose(0, 1, 3, 2, 4).reshape(N_ZERO * NBG, B, B)
    owner_of = owners[:, :, 0]
    positions = jnp.arange(NBG, dtype=jnp.int32)
    same_owner = (owner_of[:, :, None] == owner_of[:, None, :]) & (positions[None, None, :] < positions[None, :, None])
    slot_of = lax.optimization_barrier(jnp.sum(same_owner.astype(jnp.int32), axis=2))
    home_index = (owner_of * SLOTS + slot_of).reshape(N_ZERO * NBG).astype(jnp.int32)
    group_index = jnp.repeat(jnp.arange(N_ZERO, dtype=jnp.int32), NBG)
    left_seeds = roots[group_index, 0, home_index]
    right_seeds = roots[group_index, 1, home_index]
    factor = 0.05 * clip_scale * clip_scale

    def one_block(pieces_in):
        block, left_old, right_old, left_seed, right_seed, weight = pieces_in
        gram_left = jnp.dot(block, block.T, preferred_element_type=jnp.float32)
        gram_right = jnp.dot(block.T, block, preferred_element_type=jnp.float32)
        left_new = BETA * left_old + factor * gram_left
        right_new = BETA * right_old + factor * gram_right
        left_root = inverse_root(left_seed, left_new)
        right_root = inverse_root(right_seed, right_new)
        left_applied = jnp.dot(left_root, block, preferred_element_type=jnp.float32).astype(jnp.bfloat16)
        direction = jnp.dot(left_applied, right_root, preferred_element_type=jnp.float32).astype(jnp.bfloat16)
        direction_wide = direction.astype(jnp.float32)
        square_sum = jnp.sum(direction_wide * direction_wide)
        graft_ratio = jnp.sqrt(weight) / (jnp.sqrt(square_sum) + 1e-06)
        return (left_new, right_new, left_root, right_root, (direction_wide * graft_ratio).astype(jnp.bfloat16))
    left_new, right_new, left_root, right_root, block_update = lax.map(one_block, (blocks, left_stats.reshape(N_ZERO * NBG, B, B), right_stats.reshape(N_ZERO * NBG, B, B), left_seeds, right_seeds, adam_sq))
    new_roots = roots.at[group_index, 0, home_index].set(left_root).at[group_index, 1, home_index].set(right_root)
    update = block_update.reshape(N_ZERO, RB_DEV, CB, B, B).transpose(0, 1, 3, 2, 4).reshape(RB, B, D)
    return (update, new_second, left_new.reshape(N_ZERO, NBG, B, B), right_new.reshape(N_ZERO, NBG, B, B), new_roots)
```

```python
import functools
import math

import jax
import jax.numpy as jnp
from jax import lax
from jax.experimental import pallas as pl
from jax.experimental.pallas import tpu as pltpu
from jax.sharding import PartitionSpec as P

BETA = 0.95
VMEM_LIMIT = 56 * 1024 * 1024
VMEM = pl.BlockSpec(memory_space=pltpu.VMEM)
SMEM = pl.BlockSpec(memory_space=pltpu.SMEM)
PARAMS = pltpu.CompilerParams(vmem_limit_bytes=VMEM_LIMIT)


def dot(former, latter):
    return jnp.dot(former, latter, preferred_element_type=jnp.float32)


def split(wide):
    high = wide.astype(jnp.bfloat16)
    return high, (wide - high.astype(jnp.float32)).astype(jnp.bfloat16)


def grams_of(block):
    left = lax.dot_general(
        block, block, (((1,), (1,)), ((), ())), preferred_element_type=jnp.float32
    )
    right = lax.dot_general(
        block, block, (((0,), (0,)), ((), ())), preferred_element_type=jnp.float32
    )
    return left, right


def pack_kernel(slots, me_ref, owner_ref, grads_ref, left_ref, right_ref, out_ref, taken_ref):
    rows_dev, rows, width = grads_ref.shape
    order = left_ref.shape[-1]
    cols = width // order
    for owner in range(out_ref.shape[0]):
        taken_ref[owner] = 0
    row = me_ref[0] * rows + lax.broadcasted_iota(jnp.int32, (rows, order), 0)
    lower = lax.broadcasted_iota(jnp.int32, (rows, order), 1) <= row
    for k in range(rows_dev * cols):
        owner = owner_ref[k]
        slot = taken_ref[owner]
        taken_ref[owner] = slot + 1
        piece = grads_ref[k // cols, :, (k % cols) * order : (k % cols + 1) * order]
        out_ref[owner, slot] = piece
        out_ref[k, 2 * slots] = piece
        out_ref[owner, slots + slot] = jnp.where(lower, left_ref[k], right_ref[k]).astype(
            jnp.bfloat16
        )


def tally_kernel(me_ref, grads_ref, right_ref, _, square_ref, diagonal_ref):
    rows_dev, rows, width = grads_ref.shape
    blocks, _, order = right_ref.shape
    total = jnp.zeros((8, order), jnp.float32)
    for i in range(rows_dev):
        for half in range(width // order):
            wide = grads_ref[i, :, half * order : (half + 1) * order].astype(jnp.float32)
            wide = wide * wide
            total = total + wide[:8] + wide[8:]
    square_ref[...] = jnp.broadcast_to(jnp.sum(total, keepdims=True), square_ref.shape)
    row = me_ref[0] * rows + lax.broadcasted_iota(jnp.int32, (rows, order), 0)
    mine = lax.broadcasted_iota(jnp.int32, (rows, order), 1) == row
    for k in range(blocks):
        diagonal_ref[pl.ds(k, 1), :] = jnp.sum(
            jnp.where(mine, right_ref[k], 0.0), axis=0, keepdims=True
        )


def fifth_kernel(seed_ref, high_ref, low_ref):
    seed = seed_ref[0]
    high, low = split(dot(seed, seed))
    high, low = split(dot(high, high) + (dot(high, low) + dot(low, high)))
    high, low = split(dot(seed, high) + dot(seed, low))
    high_ref[0] = high
    low_ref[0] = low


def gram_kernel(block_ref, out_ref):
    devices, _, rows, order = block_ref.shape
    left, right = grams_of(block_ref[...].reshape(devices * rows, order))
    out_ref[:, 0] = left.reshape(devices, rows, order).astype(jnp.bfloat16)
    out_ref[:, 1] = right.reshape(devices, rows, order).astype(jnp.bfloat16)


def owner_kernel(
    me_ref,
    owner_ref,
    factor_ref,
    block_ref,
    mixed_ref,
    seed_ref,
    high_ref,
    low_ref,
    diagonal_ref,
    roots_ref,
    out_ref,
):
    slot = pl.program_id(0)
    devices, _, rows, order = block_ref.shape
    me = me_ref[0]
    load, chosen = jnp.int32(0), jnp.int32(0)
    for k in range(diagonal_ref.shape[0]):
        mine = owner_ref[k] == me
        chosen = jnp.where(mine & (load == slot), k, chosen)
        load = load + mine.astype(jnp.int32)
    live = slot < load
    factor = factor_ref[0]
    block = block_ref[...].reshape(order, order)
    mixed = mixed_ref[...].reshape(order, order).astype(jnp.float32)
    turned = mixed.T
    row = lax.broadcasted_iota(jnp.int32, (order, order), 0)
    col = lax.broadcasted_iota(jnp.int32, (order, order), 1)
    diagonal = diagonal_ref[pl.ds(chosen, 1), :]
    left_old = jnp.where(col <= row, mixed, turned)
    right_old = jnp.where(col > row, mixed, jnp.where(col == row, diagonal, turned))
    left_gram, right_gram = grams_of(block)

    def new_root(side, old, gram):
        high, low = split(BETA * old + factor * gram)
        fifth_high, fifth_low = high_ref[side, 0], low_ref[side, 0]
        moved = dot(fifth_high, high) + (dot(fifth_high, low) + dot(fifth_low, high))
        seed = seed_ref[side, 0]
        root = (1.25 * seed.astype(jnp.float32) - 0.25 * moved).astype(jnp.bfloat16)
        roots_ref[side, 0] = jnp.where(live, root, seed)
        return root

    left_root = new_root(0, left_old, left_gram)
    right_root = new_root(1, right_old, right_gram)
    applied = dot(left_root, block).astype(jnp.bfloat16)
    direction = dot(applied, right_root).astype(jnp.bfloat16).astype(jnp.float32)
    norm = jnp.sqrt(jnp.sum(direction * direction, keepdims=True)) + 1e-06
    out_ref[...] = (direction / norm).astype(jnp.bfloat16).reshape(out_ref.shape)


def place_kernel(owner_ref, norm_ref, back_ref, out_ref, taken_ref):
    rows_dev, rows, width = out_ref.shape
    order = back_ref.shape[-1]
    cols = width // order
    for owner in range(back_ref.shape[0]):
        taken_ref[owner] = 0
    for k in range(rows_dev * cols):
        owner = owner_ref[k]
        slot = taken_ref[owner]
        taken_ref[owner] = slot + 1
        out_ref[k // cols, :, (k % cols) * order : (k % cols + 1) * order] = (
            back_ref[owner, slot].astype(jnp.float32) * norm_ref[k]
        ).astype(jnp.bfloat16)


def butterfly(values, axis):
    size = lax.axis_size(axis)
    step = 1
    while step < size:
        values = values + lax.ppermute(values, axis, [(i, i ^ step) for i in range(size)])
        step *= 2
    return values


def exchange(values):
    return lax.all_to_all(values, "blk", split_axis=0, concat_axis=0, tiled=True)


def cost(passes, order, moved):
    return pl.CostEstimate(
        flops=2 * passes * order**3, bytes_accessed=moved, transcendentals=0
    )


def local(grads, owners, left_stats, right_stats, second_moment, roots):
    devices = lax.axis_size("blk")
    rows_dev, rows, width = grads.shape
    order = left_stats.shape[-1]
    cols = width // order
    blocks = rows_dev * cols
    slots = roots.shape[2]
    pieces = 2 * slots + 1
    me = lax.axis_index("blk").astype(jnp.int32).reshape(1)
    owner_of = owners.reshape(blocks)
    left_old, right_old = left_stats[0], right_stats[0]
    taken = [pltpu.SMEM((devices,), jnp.int32)]

    sent = pl.pallas_call(
        functools.partial(pack_kernel, slots),
        out_shape=jax.ShapeDtypeStruct((devices, pieces, rows, order), jnp.bfloat16),
        in_specs=[SMEM, SMEM, VMEM, VMEM, VMEM],
        out_specs=VMEM,
        scratch_shapes=taken,
        compiler_params=PARAMS,
        name="pack",
    )(me, owner_of, grads, left_old, right_old)
    arrived = exchange(sent)

    square, diagonal = pl.pallas_call(
        tally_kernel,
        out_shape=[
            jax.ShapeDtypeStruct((8, order), jnp.float32),
            jax.ShapeDtypeStruct((blocks, order), jnp.float32),
        ],
        in_specs=[SMEM, VMEM, VMEM, pl.BlockSpec(memory_space=pl.ANY)],
        out_specs=[VMEM, VMEM],
        compiler_params=PARAMS,
        name="tally",
    )(me, grads, right_old, sent)
    square = butterfly(square, "zero")
    gathered = butterfly(jnp.concatenate([diagonal, square]), "blk")
    diagonal, total = gathered[:blocks], gathered[blocks, 0]
    entries = rows_dev * lax.axis_size("zero") * order * width
    scale = jnp.minimum(1.0, math.sqrt(entries) / (jnp.sqrt(total) + 1e-06))
    factor = 0.05 * scale * scale

    seeds = roots[0]
    square_spec = pl.BlockSpec((1, order, order), lambda i: (i, 0, 0))
    fifth_shape = jax.ShapeDtypeStruct((2 * slots, order, order), jnp.bfloat16)
    high, low = pl.pallas_call(
        fifth_kernel,
        grid=(2 * slots,),
        out_shape=[fifth_shape, fifth_shape],
        in_specs=[square_spec],
        out_specs=[square_spec, square_spec],
        compiler_params=PARAMS,
        cost_estimate=cost(12 * slots, order, 12 * slots * order * order),
        name="fifth",
    )(seeds.reshape(2 * slots, order, order))
    high = high.reshape(2, slots, order, order)
    low = low.reshape(2, slots, order, order)

    clipped = grads.astype(jnp.float32) * scale
    new_second = 0.95 * second_moment + 0.05 * clipped * clipped
    adam_step = clipped / (jnp.sqrt(new_second) + 1e-08)
    adam_part = jnp.sum(
        (adam_step * adam_step).reshape(rows_dev, rows, cols, order), axis=(1, 3)
    ).reshape(blocks)
    adam_norm = jnp.sqrt(butterfly(adam_part, "blk"))

    grams = pl.pallas_call(
        gram_kernel,
        grid=(1,),
        out_shape=jax.ShapeDtypeStruct((devices, 2, rows, order), jnp.bfloat16),
        in_specs=[pl.BlockSpec((devices, 1, rows, order), lambda i: (0, 2 * slots, 0, 0))],
        out_specs=pl.BlockSpec((devices, 2, rows, order), lambda i: (0, 0, 0, 0)),
        compiler_params=PARAMS,
        cost_estimate=cost(2, order, 6 * order * order),
        name="grams",
    )(arrived)
    grams_back = exchange(grams)

    side_spec = pl.BlockSpec((2, 1, order, order), lambda s: (0, s, 0, 0))
    new_roots, update = pl.pallas_call(
        owner_kernel,
        grid=(slots,),
        out_shape=[
            jax.ShapeDtypeStruct((2, slots, order, order), jnp.bfloat16),
            jax.ShapeDtypeStruct((devices, slots, rows, order), jnp.bfloat16),
        ],
        in_specs=[
            SMEM,
            SMEM,
            SMEM,
            pl.BlockSpec((devices, 1, rows, order), lambda s: (0, s, 0, 0)),
            pl.BlockSpec((devices, 1, rows, order), lambda s: (0, slots + s, 0, 0)),
            side_spec,
            side_spec,
            side_spec,
            pl.BlockSpec((blocks, order), lambda s: (0, 0)),
        ],
        out_specs=[
            side_spec,
            pl.BlockSpec((devices, 1, rows, order), lambda s: (0, s, 0, 0)),
        ],
        compiler_params=PARAMS,
        cost_estimate=cost(10 * slots, order, 24 * slots * order * order),
        name="owner",
    )(me, owner_of, factor.reshape(1), arrived, arrived, seeds, high, low, diagonal)
    update_back = exchange(update)

    new_left = BETA * left_old + factor * grams_back[:blocks, 0].astype(jnp.float32)
    new_right = BETA * right_old + factor * grams_back[:blocks, 1].astype(jnp.float32)

    placed = pl.pallas_call(
        place_kernel,
        out_shape=jax.ShapeDtypeStruct((rows_dev, rows, width), jnp.bfloat16),
        in_specs=[SMEM, SMEM, VMEM],
        out_specs=VMEM,
        scratch_shapes=taken,
        compiler_params=PARAMS,
        name="place",
    )(owner_of, adam_norm, update_back)
    return (placed, new_second, new_left[None], new_right[None], new_roots[None])


def solution(mesh):
    placed = (
        P("zero", "blk", None),
        P("zero", None, None),
        P("zero", None, "blk", None),
        P("zero", None, "blk", None),
        P("zero", "blk", None),
        P("zero", None, "blk", None, None),
    )
    return jax.shard_map(
        local,
        mesh=mesh,
        in_specs=placed,
        out_specs=(
            P("zero", "blk", None),
            P("zero", "blk", None),
            P("zero", None, "blk", None),
            P("zero", None, "blk", None),
            P("zero", None, "blk", None, None),
        ),
        check_vma=False,
    )
```

```python
import functools
import math

import jax
import jax.numpy as jnp
from jax import lax
from jax.experimental import pallas as pl
from jax.experimental.pallas import tpu as pltpu
from jax.sharding import PartitionSpec as P

BETA = 0.95
VMEM_LIMIT = 56 * 1024 * 1024
VMEM = pl.BlockSpec(memory_space=pltpu.VMEM)
SMEM = pl.BlockSpec(memory_space=pltpu.SMEM)
PARAMS = pltpu.CompilerParams(vmem_limit_bytes=VMEM_LIMIT)


def dot(former, latter):
    return jnp.dot(former, latter, preferred_element_type=jnp.float32)


def split(wide):
    high = wide.astype(jnp.bfloat16)
    return high, (wide - high.astype(jnp.float32)).astype(jnp.bfloat16)


def grams_of(block):
    left = lax.dot_general(
        block, block, (((1,), (1,)), ((), ())), preferred_element_type=jnp.float32
    )
    right = lax.dot_general(
        block, block, (((0,), (0,)), ((), ())), preferred_element_type=jnp.float32
    )
    return left, right


LANES = 128


def thirds(wide):
    first = wide.astype(jnp.bfloat16).astype(jnp.float32)
    second = (wide - first).astype(jnp.bfloat16).astype(jnp.float32)
    return first, second, wide - first - second


def sublanes(shape):
    return lax.broadcasted_iota(jnp.int32, shape, len(shape) - 2)


def lanes(shape):
    return lax.broadcasted_iota(jnp.int32, shape, len(shape) - 1)


def store_piece(ref, place, first, piece):
    for tile in range(piece.shape[-1] // LANES):
        ref[place, first + tile] = piece[:, tile * LANES : (tile + 1) * LANES]


def whole_block(ref):
    devices, tiles, rows, _ = ref.shape
    return jnp.concatenate(
        [ref[:, tile].reshape(devices * rows, LANES) for tile in range(tiles)], axis=1
    )


def pack_kernel(slots, me_ref, owner_ref, grads_ref, left_ref, right_ref, out_ref, taken_ref):
    rows_dev, rows, width = grads_ref.shape
    order = left_ref.shape[-1]
    cols = width // order
    tiles = order // LANES
    devices, extra = out_ref.shape[0], out_ref.shape[1] - 1
    total = jnp.zeros((8, order), jnp.float32)
    for i in range(rows_dev):
        for j in range(cols):
            wide = grads_ref[i, :, j * order : (j + 1) * order].astype(jnp.float32)
            wide = wide * wide
            for part in range(rows // 8):
                total = total + wide[8 * part : 8 * part + 8]
    terms = thirds(jnp.sum(total, keepdims=True))
    tile_row = sublanes((rows, LANES))
    base = jnp.zeros((rows, LANES), jnp.float32)
    for place, term in enumerate(terms):
        base = jnp.where(tile_row == slots + place, term, base)
    for owner in range(devices):
        taken_ref[owner] = 0
        out_ref[owner, extra] = base.astype(jnp.bfloat16)
    row = me_ref[0] * rows + sublanes((rows, order))
    lower = lanes((rows, order)) <= row
    mine = lanes((rows, order)) == row
    for k in range(rows_dev * cols):
        owner = owner_ref[k]
        slot = taken_ref[owner]
        taken_ref[owner] = slot + 1
        piece = grads_ref[k // cols, :, (k % cols) * order : (k % cols + 1) * order]
        store_piece(out_ref, owner, slot * tiles, piece)
        store_piece(out_ref, k, 2 * slots * tiles, piece)
        right = right_ref[k]
        mixed = jnp.where(lower, left_ref[k], right).astype(jnp.bfloat16)
        store_piece(out_ref, owner, (slots + slot) * tiles, mixed)
        marked = jnp.where(mine, right, 0.0)
        diagonal = marked[:, :LANES]
        for tile in range(1, tiles):
            diagonal = diagonal + marked[:, tile * LANES : (tile + 1) * LANES]
        diagonal = jnp.sum(diagonal, axis=0, keepdims=True)
        out_ref[owner, extra] = jnp.where(
            tile_row == slot, diagonal, out_ref[owner, extra].astype(jnp.float32)
        ).astype(jnp.bfloat16)


def fifth_kernel(seed_ref, high_ref, low_ref):
    seed = seed_ref[0]
    high, low = split(dot(seed, seed))
    high, low = split(dot(high, high) + (dot(high, low) + dot(low, high)))
    high, low = split(dot(seed, high) + dot(seed, low))
    high_ref[0] = high
    low_ref[0] = low


def gram_kernel(slots, block_ref, extra_ref, _, out_ref, square_ref, diagonal_ref):
    devices, tiles, rows, lane_count = block_ref.shape
    order = tiles * lane_count
    for side, gram in enumerate(grams_of(whole_block(block_ref))):
        gram = gram.astype(jnp.bfloat16)
        for tile in range(tiles):
            out_ref[:, side * tiles + tile] = gram[
                :, tile * lane_count : (tile + 1) * lane_count
            ].reshape(devices, rows, lane_count)
    sums = []
    for tile in range(tiles):
        total = jnp.zeros((rows, lane_count), jnp.float32)
        for source in range(tile * devices // tiles, (tile + 1) * devices // tiles):
            total = total + extra_ref[source, 0].astype(jnp.float32)
        sums.append(total)
    tile_row = sublanes((rows, lane_count))
    for slot in range(slots):
        diagonal_ref[slot : slot + 1, :] = jnp.concatenate(
            [
                jnp.sum(jnp.where(tile_row == slot, total, 0.0), axis=0, keepdims=True)
                for total in sums
            ],
            axis=1,
        )
    total = functools.reduce(jnp.add, sums)
    terms = (tile_row >= slots) & (tile_row < slots + 3)
    square = jnp.sum(jnp.where(terms, total, 0.0), axis=0, keepdims=True)
    square_ref[...] = jnp.broadcast_to(square, square_ref.shape)


def adam_kernel(order, scale_ref, grads_ref, second_ref, new_ref, tile_ref):
    rows_dev, rows, width = grads_ref.shape
    cols = width // order
    scale = scale_ref[0]
    sums = jnp.zeros((1, LANES), jnp.float32)
    lane = lanes((1, LANES))
    for k in range(rows_dev * cols):
        where = (k // cols, slice(None), slice((k % cols) * order, (k % cols + 1) * order))
        clipped = grads_ref[where].astype(jnp.float32) * scale
        second = 0.95 * second_ref[where] + 0.05 * clipped * clipped
        new_ref[where] = second
        step = clipped / (jnp.sqrt(second) + 1e-08)
        sums = jnp.where(lane == k, jnp.sum(step * step, keepdims=True), sums)
    tile_row = sublanes(tile_ref.shape)
    tile = jnp.zeros(tile_ref.shape, jnp.float32)
    for place, term in enumerate(thirds(sums)):
        tile = jnp.where(tile_row == place, term, tile)
    tile_ref[...] = tile.astype(jnp.bfloat16)


def owner_kernel(
    me_ref,
    owner_ref,
    factor_ref,
    block_ref,
    mixed_ref,
    seed_ref,
    high_ref,
    low_ref,
    diagonal_ref,
    adam_ref,
    roots_ref,
    out_ref,
):
    slot = pl.program_id(0)
    devices, tiles, rows, lane_count = block_ref.shape
    order = tiles * lane_count
    me = me_ref[0]
    load = jnp.int32(0)
    for k in range(owner_ref.shape[0]):
        load = load + (owner_ref[k] == me).astype(jnp.int32)
    live = slot < load
    factor = factor_ref[0]
    block = whole_block(block_ref)
    mixed = whole_block(mixed_ref).astype(jnp.float32)
    turned = mixed.T
    row, col = sublanes((order, order)), lanes((order, order))
    diagonal = diagonal_ref[pl.ds(slot, 1), :]
    left_old = jnp.where(col <= row, mixed, turned)
    right_old = jnp.where(col > row, mixed, jnp.where(col == row, diagonal, turned))
    left_gram, right_gram = grams_of(block)

    def new_root(side, old, gram):
        high, low = split(BETA * old + factor * gram)
        fifth_high, fifth_low = high_ref[side, 0], low_ref[side, 0]
        moved = dot(fifth_high, high) + (dot(fifth_high, low) + dot(fifth_low, high))
        seed = seed_ref[side, 0]
        root = (1.25 * seed.astype(jnp.float32) - 0.25 * moved).astype(jnp.bfloat16)
        roots_ref[side, 0] = jnp.where(live, root, seed)
        return root

    left_root = new_root(0, left_old, left_gram)
    right_root = new_root(1, right_old, right_gram)
    applied = dot(left_root, block).astype(jnp.bfloat16)
    direction = dot(applied, right_root).astype(jnp.bfloat16).astype(jnp.float32)
    norm = jnp.sqrt(jnp.sum(direction * direction, keepdims=True)) + 1e-06
    unit = (direction / norm).astype(jnp.bfloat16)
    for tile in range(tiles):
        out_ref[:, pl.ds(slot * tiles + tile, 1)] = unit[
            :, tile * lane_count : (tile + 1) * lane_count
        ].reshape(devices, 1, rows, lane_count)

    @pl.when(slot == 0)
    def _():
        out_ref[:, out_ref.shape[1] - 1] = jnp.broadcast_to(
            adam_ref[...][None], (devices, rows, lane_count)
        )


def stats_kernel(factor_ref, left_ref, right_ref, gram_ref, new_left_ref, new_right_ref):
    factor = factor_ref[0]
    tiles = gram_ref.shape[1] // 2
    for side, (old_ref, new_ref) in enumerate(
        ((left_ref, new_left_ref), (right_ref, new_right_ref))
    ):
        for tile in range(tiles):
            part = slice(tile * LANES, (tile + 1) * LANES)
            new_ref[:, :, part] = BETA * old_ref[:, :, part] + factor * gram_ref[
                :, side * tiles + tile
            ].astype(jnp.float32)


def place_kernel(order, owner_ref, back_ref, out_ref, taken_ref):
    rows_dev, rows, width = out_ref.shape
    cols = width // order
    tiles = order // LANES
    devices, extra = back_ref.shape[0], back_ref.shape[1] - 1
    total = jnp.zeros((rows, LANES), jnp.float32)
    for source in range(devices):
        taken_ref[source] = 0
        total = total + back_ref[source, extra].astype(jnp.float32)
    norms = jnp.sqrt(jnp.sum(total, axis=0, keepdims=True))
    lane = lanes((1, LANES))
    for k in range(rows_dev * cols):
        owner = owner_ref[k]
        slot = taken_ref[owner]
        taken_ref[owner] = slot + 1
        norm = jnp.sum(jnp.where(lane == k, norms, 0.0), axis=1, keepdims=True)
        for tile in range(tiles):
            first = (k % cols) * order + tile * LANES
            out_ref[k // cols, :, first : first + LANES] = (
                back_ref[owner, slot * tiles + tile].astype(jnp.float32) * norm
            ).astype(jnp.bfloat16)


def butterfly(values, axis):
    size = lax.axis_size(axis)
    step = 1
    while step < size:
        values = values + lax.ppermute(values, axis, [(i, i ^ step) for i in range(size)])
        step *= 2
    return values


def exchange(values):
    return lax.all_to_all(values, "blk", split_axis=0, concat_axis=0, tiled=True)


def cost(passes, order, moved):
    return pl.CostEstimate(
        flops=2 * passes * order**3, bytes_accessed=moved, transcendentals=0
    )


def local(grads, owners, left_stats, right_stats, second_moment, roots):
    devices = lax.axis_size("blk")
    rows_dev, rows, width = grads.shape
    order = left_stats.shape[-1]
    cols = width // order
    blocks = rows_dev * cols
    slots = roots.shape[2]
    tiles = order // LANES
    me = lax.axis_index("blk").astype(jnp.int32).reshape(1)
    owner_of = owners.reshape(blocks)
    left_old, right_old = left_stats[0], right_stats[0]
    taken = [pltpu.SMEM((devices,), jnp.int32)]

    sent = pl.pallas_call(
        functools.partial(pack_kernel, slots),
        out_shape=jax.ShapeDtypeStruct(
            (devices, (2 * slots + 1) * tiles + 1, rows, LANES), jnp.bfloat16
        ),
        in_specs=[SMEM, SMEM, VMEM, VMEM, VMEM],
        out_specs=VMEM,
        scratch_shapes=taken,
        compiler_params=PARAMS,
        name="pack",
    )(me, owner_of, grads, left_old, right_old)
    arrived = exchange(sent)

    seeds = roots[0]
    square_spec = pl.BlockSpec((1, order, order), lambda i: (i, 0, 0))
    fifth_shape = jax.ShapeDtypeStruct((2 * slots, order, order), jnp.bfloat16)
    high, low = pl.pallas_call(
        fifth_kernel,
        grid=(2 * slots,),
        out_shape=[fifth_shape, fifth_shape],
        in_specs=[square_spec],
        out_specs=[square_spec, square_spec],
        compiler_params=PARAMS,
        cost_estimate=cost(12 * slots, order, 12 * slots * order * order),
        name="fifth",
    )(seeds.reshape(2 * slots, order, order))

    grams, square, diagonal = pl.pallas_call(
        functools.partial(gram_kernel, slots),
        grid=(1,),
        out_shape=[
            jax.ShapeDtypeStruct((devices, 2 * tiles, rows, LANES), jnp.bfloat16),
            jax.ShapeDtypeStruct((8, LANES), jnp.float32),
            jax.ShapeDtypeStruct((slots, order), jnp.float32),
        ],
        in_specs=[
            pl.BlockSpec((devices, tiles, rows, LANES), lambda i: (0, 2 * slots, 0, 0)),
            pl.BlockSpec(
                (devices, 1, rows, LANES), lambda i: (0, (2 * slots + 1) * tiles, 0, 0)
            ),
            pl.BlockSpec(memory_space=pl.ANY),
        ],
        out_specs=[
            pl.BlockSpec((devices, 2 * tiles, rows, LANES), lambda i: (0, 0, 0, 0)),
            pl.BlockSpec((8, LANES), lambda i: (0, 0)),
            pl.BlockSpec((slots, order), lambda i: (0, 0)),
        ],
        compiler_params=PARAMS,
        cost_estimate=cost(2, order, 6 * order * order),
        name="grams",
    )(arrived, arrived, low)
    grams_back = exchange(grams)

    total = butterfly(square, "zero")[0, 0]
    entries = rows_dev * lax.axis_size("zero") * order * width
    scale = jnp.minimum(1.0, math.sqrt(entries) / (jnp.sqrt(total) + 1e-06))
    factor = 0.05 * scale * scale
    new_second, adam = pl.pallas_call(
        functools.partial(adam_kernel, order),
        out_shape=[
            jax.ShapeDtypeStruct(second_moment.shape, jnp.float32),
            jax.ShapeDtypeStruct((rows, LANES), jnp.bfloat16),
        ],
        in_specs=[SMEM, VMEM, VMEM],
        out_specs=[VMEM, VMEM],
        compiler_params=PARAMS,
        name="adam",
    )(scale.reshape(1), grads, second_moment)
    side_spec = pl.BlockSpec((2, 1, order, order), lambda s: (0, s, 0, 0))
    new_roots, update = pl.pallas_call(
        owner_kernel,
        grid=(slots,),
        out_shape=[
            jax.ShapeDtypeStruct((2, slots, order, order), jnp.bfloat16),
            jax.ShapeDtypeStruct((devices, slots * tiles + 1, rows, LANES), jnp.bfloat16),
        ],
        in_specs=[
            SMEM,
            SMEM,
            SMEM,
            pl.BlockSpec((devices, tiles, rows, LANES), lambda s: (0, s, 0, 0)),
            pl.BlockSpec((devices, tiles, rows, LANES), lambda s: (0, slots + s, 0, 0)),
            side_spec,
            side_spec,
            side_spec,
            pl.BlockSpec((slots, order), lambda s: (0, 0)),
            pl.BlockSpec((rows, LANES), lambda s: (0, 0)),
        ],
        out_specs=[
            side_spec,
            pl.BlockSpec((devices, slots * tiles + 1, rows, LANES), lambda s: (0, 0, 0, 0)),
        ],
        compiler_params=PARAMS,
        cost_estimate=cost(10 * slots, order, 24 * slots * order * order),
        name="owner",
    )(
        me,
        owner_of,
        factor.reshape(1),
        arrived,
        arrived,
        seeds,
        high.reshape(2, slots, order, order),
        low.reshape(2, slots, order, order),
        diagonal,
        adam,
    )
    update_back = exchange(update)

    new_left, new_right = pl.pallas_call(
        stats_kernel,
        grid=(blocks // 4,),
        out_shape=[jax.ShapeDtypeStruct(left_old.shape, jnp.float32)] * 2,
        in_specs=[
            SMEM,
            pl.BlockSpec((4, rows, order), lambda i: (i, 0, 0)),
            pl.BlockSpec((4, rows, order), lambda i: (i, 0, 0)),
            pl.BlockSpec((4, 2 * tiles, rows, LANES), lambda i: (i, 0, 0, 0)),
        ],
        out_specs=[pl.BlockSpec((4, rows, order), lambda i: (i, 0, 0))] * 2,
        compiler_params=PARAMS,
        name="stats",
    )(factor.reshape(1), left_old, right_old, grams_back)

    placed = pl.pallas_call(
        functools.partial(place_kernel, order),
        out_shape=jax.ShapeDtypeStruct((rows_dev, rows, width), jnp.bfloat16),
        in_specs=[SMEM, VMEM],
        out_specs=VMEM,
        scratch_shapes=taken,
        compiler_params=PARAMS,
        name="place",
    )(owner_of, update_back)
    return (placed, new_second, new_left[None], new_right[None], new_roots[None])


def solution(mesh):
    placed = (
        P("zero", "blk", None),
        P("zero", None, None),
        P("zero", None, "blk", None),
        P("zero", None, "blk", None),
        P("zero", "blk", None),
        P("zero", None, "blk", None, None),
    )
    return jax.shard_map(
        local,
        mesh=mesh,
        in_specs=placed,
        out_specs=(
            P("zero", "blk", None),
            P("zero", "blk", None),
            P("zero", None, "blk", None),
            P("zero", None, "blk", None),
            P("zero", None, "blk", None, None),
        ),
        check_vma=False,
    )
```

```python
import functools
import math

import jax
import jax.numpy as jnp
from jax import lax
from jax.experimental import pallas as pl
from jax.experimental.pallas import tpu as pltpu
from jax.sharding import PartitionSpec as P

BETA = 0.95
VMEM_LIMIT = 56 * 1024 * 1024
VMEM = pl.BlockSpec(memory_space=pltpu.VMEM)
SMEM = pl.BlockSpec(memory_space=pltpu.SMEM)
PARAMS = pltpu.CompilerParams(vmem_limit_bytes=VMEM_LIMIT)


def dot(former, latter):
    return jnp.dot(former, latter, preferred_element_type=jnp.float32)


def split(wide):
    high = wide.astype(jnp.bfloat16)
    return high, (wide - high.astype(jnp.float32)).astype(jnp.bfloat16)


LANES = 128


def sublanes(shape):
    return lax.broadcasted_iota(jnp.int32, shape, len(shape) - 2)


def lanes(shape):
    return lax.broadcasted_iota(jnp.int32, shape, len(shape) - 1)


def store_piece(ref, place, first, piece):
    for tile in range(piece.shape[-1] // LANES):
        ref[place, first + tile] = piece[:, tile * LANES : (tile + 1) * LANES]


def whole_block(ref):
    devices, tiles, rows, _ = ref.shape
    return jnp.concatenate(
        [ref[:, tile].reshape(devices * rows, LANES) for tile in range(tiles)], axis=1
    )


OWNER, HELPER, SPARE = 0, 1, 2


class Plan:
    def __init__(self, ref, blocks, devices):
        self.ref, self.blocks, self.devices = ref, blocks, devices

    @staticmethod
    def size(blocks, devices):
        return 3 * blocks + 3 * devices + 4

    def at(self, part, index):
        blocks, devices = self.blocks, self.devices
        start = {
            "slot": 0,
            "single": blocks,
            "owner": 2 * blocks,
            "load": 3 * blocks,
            "helper": 3 * blocks + devices,
            "idle": 3 * blocks + 2 * devices,
            "role": 3 * blocks + 3 * devices + 1,
            "own": 3 * blocks + 3 * devices + 2,
        }[part]
        return start + index

    def get(self, part, index=0):
        return self.ref[self.at(part, index)]

    def put(self, part, index, value):
        self.ref[self.at(part, index)] = value

    def share(self):
        return self.blocks // (self.devices - self.blocks)

    def spare_of(self, block):
        return self.get("idle", block // self.share())

    def fill(self, owner_ref, me):
        blocks, devices = self.blocks, self.devices
        spares = devices - blocks
        for device in range(devices):
            self.put("load", device, 0)
        for k in range(blocks):
            owner = owner_ref[k]
            slot = self.get("load", owner)
            self.put("owner", k, owner)
            self.put("slot", k, slot)
            self.put("load", owner, slot + 1)
        count, role = jnp.int32(0), jnp.int32(OWNER)
        for device in range(devices):
            idle = self.get("load", device) == 0
            self.put("idle", count, device)
            kind = jnp.where(count < spares, SPARE, HELPER)
            role = jnp.where(idle & (me == device), kind, role)
            count = count + idle.astype(jnp.int32)
        count = jnp.int32(spares)
        for device in range(devices):
            double = self.get("load", device) == 2
            helper = self.get("idle", jnp.minimum(count, devices - 1))
            self.put("helper", device, jnp.where(double, helper, device))
            count = count + double.astype(jnp.int32)
        for k in range(blocks):
            load = self.get("load", self.get("owner", k))
            self.put("single", k, (load == 1).astype(jnp.int32))
        self.put("role", 0, role)
        self.put("own", 0, self.get("load", me))


def pack_kernel(slots, me_ref, owner_ref, grads_ref, left_ref, right_ref, out_ref, plan_ref):
    rows_dev, rows, width = grads_ref.shape
    order = left_ref.shape[-1]
    cols = width // order
    blocks = rows_dev * cols
    tiles = order // LANES
    devices, extra = out_ref.shape[0], out_ref.shape[1] - 1
    me = me_ref[0]
    plan = Plan(plan_ref, blocks, devices)
    plan.fill(owner_ref, me)
    tile_row = sublanes((rows, LANES))
    for owner in range(devices):
        out_ref[owner, extra] = jnp.zeros((rows, LANES), jnp.bfloat16)
    row = me * rows + sublanes((rows, order))
    lower = lanes((rows, order)) <= row
    mine = lanes((rows, order)) == row
    for k in range(blocks):
        owner, slot = plan.get("owner", k), plan.get("slot", k)
        piece = grads_ref[k // cols, :, (k % cols) * order : (k % cols + 1) * order]
        store_piece(out_ref, owner, slot * tiles, piece)
        store_piece(out_ref, plan.get("helper", owner), slot * tiles, piece)
        store_piece(out_ref, plan.spare_of(k), k % plan.share() * tiles, piece)
        right = right_ref[k]
        mixed = jnp.where(lower, left_ref[k], right).astype(jnp.bfloat16)
        store_piece(out_ref, owner, (slots + slot) * tiles, mixed)
        marked = jnp.where(mine, right, 0.0)
        diagonal = marked[:, :LANES]
        for tile in range(1, tiles):
            diagonal = diagonal + marked[:, tile * LANES : (tile + 1) * LANES]
        diagonal = jnp.sum(diagonal, axis=0, keepdims=True)
        out_ref[owner, extra] = jnp.where(
            tile_row == slot, diagonal, out_ref[owner, extra].astype(jnp.float32)
        ).astype(jnp.bfloat16)


def square_kernel(grads_ref, _, __, out_ref):
    rows_dev, rows, width = grads_ref.shape
    total = jnp.zeros((8, 4 * LANES), jnp.float32)
    for i in range(rows_dev):
        for part in range(width // (4 * LANES)):
            wide = grads_ref[i, :, part * 4 * LANES : (part + 1) * 4 * LANES].astype(jnp.float32)
            wide = wide * wide
            for half in range(rows // 8):
                total = total + wide[8 * half : 8 * half + 8]
    out_ref[...] = jnp.broadcast_to(jnp.sum(total, keepdims=True), out_ref.shape)


def fifth_kernel(seed_ref, high_ref, low_ref):
    seed = seed_ref[0]
    high, low = split(dot(seed, seed))
    high, low = split(dot(high, high) + (dot(high, low) + dot(low, high)))
    high, low = split(dot(seed, high) + dot(seed, low))
    high_ref[0] = high
    low_ref[0] = low


def adam_kernel(order, scale_ref, grads_ref, second_ref, _, new_ref, sums_ref):
    rows_dev, rows, width = grads_ref.shape
    cols = width // order
    scale = scale_ref[0]
    sums = jnp.zeros((1, LANES), jnp.float32)
    lane = lanes((1, LANES))
    for k in range(rows_dev * cols):
        where = (k // cols, slice(None), slice((k % cols) * order, (k % cols + 1) * order))
        clipped = grads_ref[where].astype(jnp.float32) * scale
        second = 0.95 * second_ref[where] + 0.05 * clipped * clipped
        new_ref[where] = second
        step = clipped / (jnp.sqrt(second) + 1e-08)
        sums = jnp.where(lane == k, jnp.sum(step * step, keepdims=True), sums)
    sums_ref[...] = jnp.broadcast_to(sums, sums_ref.shape)


def owner_kernel(
    blocks,
    plan_ref,
    factor_ref,
    block_ref,
    mixed_ref,
    seed_ref,
    high_ref,
    low_ref,
    extra_ref,
    roots_ref,
    out_ref,
):
    slot = pl.program_id(0)
    devices, tiles, rows, lane_count = block_ref.shape
    order = tiles * lane_count
    plan = Plan(plan_ref, blocks, devices)
    role, load = plan.get("role"), plan.get("own")
    live = slot < load
    factor = factor_ref[0]

    def put(first, value):
        value = value.astype(jnp.bfloat16)
        for tile in range(value.shape[1] // lane_count):
            out_ref[:, pl.ds(first + tile, 1)] = value[
                :, tile * lane_count : (tile + 1) * lane_count
            ].reshape(devices, 1, rows, lane_count)

    def right_gram(block):
        return lax.dot_general(
            block, block, (((0,), (0,)), ((), ())), preferred_element_type=jnp.float32
        )

    def left_part(block, start, stop):
        return lax.dot_general(
            block,
            block[start:stop],
            (((1,), (1,)), ((), ())),
            preferred_element_type=jnp.float32,
        )

    @pl.when(live)
    def _():
        block = whole_block(block_ref)
        mixed = whole_block(mixed_ref).astype(jnp.float32)
        turned = mixed.T
        row, col = sublanes((order, order)), lanes((order, order))
        diagonal = []
        tile_row = sublanes((rows, lane_count))
        for tile in range(tiles):
            total = jnp.zeros((rows, lane_count), jnp.float32)
            for source in range(tile * devices // tiles, (tile + 1) * devices // tiles):
                total = total + extra_ref[source, 0].astype(jnp.float32)
            diagonal.append(
                jnp.sum(jnp.where(tile_row == slot, total, 0.0), axis=0, keepdims=True)
            )
        diagonal = jnp.concatenate(diagonal, axis=1)
        left_old = jnp.where(col <= row, mixed, turned)
        right_old = jnp.where(col > row, mixed, jnp.where(col == row, diagonal, turned))
        left, right = left_part(block, 0, order), right_gram(block)

        def new_root(side, old, gram):
            high, low = split(BETA * old + factor * gram)
            fifth_high, fifth_low = high_ref[side, 0], low_ref[side, 0]
            moved = dot(fifth_high, high) + (dot(fifth_high, low) + dot(fifth_low, high))
            seed = seed_ref[side, 0]
            root = (1.25 * seed.astype(jnp.float32) - 0.25 * moved).astype(jnp.bfloat16)
            roots_ref[side, 0] = root
            return root

        left_root = new_root(0, left_old, left)
        right_root = new_root(1, right_old, right)
        applied = dot(left_root, block).astype(jnp.bfloat16)
        direction = dot(applied, right_root).astype(jnp.bfloat16).astype(jnp.float32)
        norm = jnp.sqrt(jnp.sum(direction * direction, keepdims=True)) + 1e-06
        put(slot * tiles, direction / norm)

        @pl.when(slot == 0)
        def _():
            put(2 * tiles, left[:, :lane_count])

        @pl.when(load == 1)
        def _():
            put(tiles, right)

    @pl.when(jnp.logical_not(live))
    def _():
        roots_ref[...] = seed_ref[...]

    @pl.when(role == HELPER)
    def _():
        block = whole_block(block_ref)
        put(slot * tiles, right_gram(block))

        @pl.when(slot == 1)
        def _():
            put(2 * tiles, left_part(block, 0, lane_count))

    @pl.when(role == SPARE)
    def _():
        put(slot * (tiles - 1), left_part(whole_block(block_ref), lane_count, order))

        @pl.when(slot == 0)
        def _():
            put(2 * (tiles - 1), left_part(whole_block(mixed_ref), lane_count, order))


def finish_kernel(
    plan_ref,
    factor_ref,
    left_ref,
    right_ref,
    back_ref,
    sums_ref,
    out_ref,
    new_left_ref,
    new_right_ref,
):
    rows_dev, rows, width = out_ref.shape
    blocks, _, order = left_ref.shape
    cols = width // order
    tiles = order // LANES
    plan = Plan(plan_ref, blocks, back_ref.shape[0])
    factor = factor_ref[0]
    norms = jnp.sqrt(sums_ref[:1, :])
    lane = lanes((1, LANES))
    for k in range(blocks):
        owner, slot = plan.get("owner", k), plan.get("slot", k)
        helper, single = plan.get("helper", owner), plan.get("single", k)
        spare = plan.spare_of(k)
        norm = jnp.sum(jnp.where(lane == k, norms, 0.0), axis=1, keepdims=True)
        right_from = jnp.where(single == 1, 1, slot) * tiles
        for tile in range(tiles):
            part = slice(tile * LANES, (tile + 1) * LANES)
            first = (k % cols) * order + tile * LANES
            out_ref[k // cols, :, first : first + LANES] = (
                back_ref[owner, slot * tiles + tile].astype(jnp.float32) * norm
            ).astype(jnp.bfloat16)
            if tile == 0:
                gram = back_ref[jnp.where(slot == 0, owner, helper), 2 * tiles]
            else:
                gram = back_ref[spare, k % plan.share() * (tiles - 1) + tile - 1]
            new_left_ref[k, :, part] = BETA * left_ref[k, :, part] + factor * gram.astype(
                jnp.float32
            )
            gram = back_ref[helper, right_from + tile]
            new_right_ref[k, :, part] = BETA * right_ref[k, :, part] + factor * gram.astype(
                jnp.float32
            )


def butterfly(values, axis, steps):
    size = lax.axis_size(axis)
    for step in steps:
        values = values + lax.ppermute(values, axis, [(i, i ^ step) for i in range(size)])
    return values


def blk_sum(values, axis, bit):
    size, width, near, halves = lax.axis_size("blk"), lax.axis_size("zero"), 4, 2
    values = butterfly(values, "blk", (1, 2))
    parts = []
    for turn in range(size // near // halves):
        pairs = []
        for place in range(size):
            for group in range(width):
                upper = ((place if axis == "blk" else group) // bit) % 2
                shift = near * (turn + upper * (size // near // halves))
                source = (place + shift) % size
                pairs.append((source * width + group, place * width + group))
        parts.append(lax.ppermute(values, ("blk", "zero"), pairs))
    return butterfly(functools.reduce(jnp.add, parts), axis, (bit,))


def exchange(values):
    return lax.all_to_all(values, "blk", split_axis=0, concat_axis=0, tiled=True)


def cost(passes, order, moved):
    return pl.CostEstimate(
        flops=2 * passes * order**3, bytes_accessed=moved, transcendentals=0
    )


def local(grads, owners, left_stats, right_stats, second_moment, roots):
    devices = lax.axis_size("blk")
    rows_dev, rows, width = grads.shape
    order = left_stats.shape[-1]
    cols = width // order
    blocks = rows_dev * cols
    slots = roots.shape[2]
    tiles = order // LANES
    me = lax.axis_index("blk").astype(jnp.int32).reshape(1)
    owner_of = owners.reshape(blocks)
    left_old, right_old = left_stats[0], right_stats[0]

    sent, plan = pl.pallas_call(
        functools.partial(pack_kernel, slots),
        out_shape=[
            jax.ShapeDtypeStruct((devices, 2 * slots * tiles + 1, rows, LANES), jnp.bfloat16),
            jax.ShapeDtypeStruct((Plan.size(blocks, devices),), jnp.int32),
        ],
        in_specs=[SMEM, SMEM, VMEM, VMEM, VMEM],
        out_specs=[VMEM, SMEM],
        compiler_params=PARAMS,
        name="pack",
    )(me, owner_of, grads, left_old, right_old)
    arrived = exchange(sent)

    seeds = roots[0]
    square_spec = pl.BlockSpec((1, order, order), lambda i: (i, 0, 0))
    fifth_shape = jax.ShapeDtypeStruct((2 * slots, order, order), jnp.bfloat16)
    high, low = pl.pallas_call(
        fifth_kernel,
        grid=(2 * slots,),
        out_shape=[fifth_shape, fifth_shape],
        in_specs=[square_spec],
        out_specs=[square_spec, square_spec],
        compiler_params=PARAMS,
        cost_estimate=cost(12 * slots, order, 12 * slots * order * order),
        name="fifth",
    )(seeds.reshape(2 * slots, order, order))
    square = pl.pallas_call(
        square_kernel,
        out_shape=jax.ShapeDtypeStruct((8, LANES), jnp.float32),
        in_specs=[VMEM, pl.BlockSpec(memory_space=pl.ANY), pl.BlockSpec(memory_space=pl.ANY)],
        out_specs=VMEM,
        compiler_params=PARAMS,
        name="square",
    )(grads, low, sent)
    total = blk_sum(butterfly(square, "zero", (1, 2, 4)), "zero", 1)[0, 0]
    entries = rows_dev * lax.axis_size("zero") * order * width
    scale = jnp.minimum(1.0, math.sqrt(entries) / (jnp.sqrt(total) + 1e-06))
    factor = (0.05 * scale * scale).reshape(1)

    side_spec = pl.BlockSpec((2, 1, order, order), lambda s: (0, s, 0, 0))
    out_tiles = 2 * tiles + 1
    new_roots, returned = pl.pallas_call(
        functools.partial(owner_kernel, blocks),
        grid=(slots,),
        out_shape=[
            jax.ShapeDtypeStruct((2, slots, order, order), jnp.bfloat16),
            jax.ShapeDtypeStruct((devices, out_tiles, rows, LANES), jnp.bfloat16),
        ],
        in_specs=[
            SMEM,
            SMEM,
            pl.BlockSpec((devices, tiles, rows, LANES), lambda s: (0, s, 0, 0)),
            pl.BlockSpec((devices, tiles, rows, LANES), lambda s: (0, slots + s, 0, 0)),
            side_spec,
            side_spec,
            side_spec,
            pl.BlockSpec((devices, 1, rows, LANES), lambda s: (0, 2 * slots * tiles, 0, 0)),
        ],
        out_specs=[
            side_spec,
            pl.BlockSpec((devices, out_tiles, rows, LANES), lambda s: (0, 0, 0, 0)),
        ],
        compiler_params=PARAMS,
        cost_estimate=cost(10 * slots, order, 24 * slots * order * order),
        name="owner",
    )(
        plan,
        factor,
        arrived,
        arrived,
        seeds,
        high.reshape(2, slots, order, order),
        low.reshape(2, slots, order, order),
        arrived,
    )
    back = exchange(returned)

    new_second, sums = pl.pallas_call(
        functools.partial(adam_kernel, order),
        out_shape=[
            jax.ShapeDtypeStruct(second_moment.shape, jnp.float32),
            jax.ShapeDtypeStruct((8, LANES), jnp.float32),
        ],
        in_specs=[SMEM, VMEM, VMEM, pl.BlockSpec(memory_space=pl.ANY)],
        out_specs=[VMEM, VMEM],
        compiler_params=PARAMS,
        name="adam",
    )(scale.reshape(1), grads, second_moment, returned)
    sums = blk_sum(sums, "blk", 1)

    placed, new_left, new_right = pl.pallas_call(
        finish_kernel,
        out_shape=[
            jax.ShapeDtypeStruct((rows_dev, rows, width), jnp.bfloat16),
            jax.ShapeDtypeStruct(left_old.shape, jnp.float32),
            jax.ShapeDtypeStruct(right_old.shape, jnp.float32),
        ],
        in_specs=[SMEM, SMEM, VMEM, VMEM, VMEM, VMEM],
        out_specs=[VMEM, VMEM, VMEM],
        compiler_params=PARAMS,
        name="finish",
    )(plan, factor, left_old, right_old, back, sums)
    return (placed, new_second, new_left[None], new_right[None], new_roots[None])


def solution(mesh):
    placed = (
        P("zero", "blk", None),
        P("zero", None, None),
        P("zero", None, "blk", None),
        P("zero", None, "blk", None),
        P("zero", "blk", None),
        P("zero", None, "blk", None, None),
    )
    return jax.shard_map(
        local,
        mesh=mesh,
        in_specs=placed,
        out_specs=(
            P("zero", "blk", None),
            P("zero", "blk", None),
            P("zero", None, "blk", None),
            P("zero", None, "blk", None),
            P("zero", None, "blk", None, None),
        ),
        check_vma=False,
    )
```

```python
import functools
import math

import jax
import jax.numpy as jnp
from jax import lax
from jax.experimental import pallas as pl
from jax.experimental.pallas import tpu as pltpu
from jax.sharding import PartitionSpec as P

BETA = 0.95
VMEM = pl.BlockSpec(memory_space=pltpu.VMEM)
SMEM = pl.BlockSpec(memory_space=pltpu.SMEM)
ANY = pl.BlockSpec(memory_space=pl.ANY)


def grant(mebibytes):
    return pltpu.CompilerParams(vmem_limit_bytes=mebibytes * 1024 * 1024)


def dot(former, latter):
    return jnp.dot(former, latter, preferred_element_type=jnp.float32)


def split(wide):
    high = wide.astype(jnp.bfloat16)
    return high, (wide - high.astype(jnp.float32)).astype(jnp.bfloat16)


LANES = 128
HBM = pl.BlockSpec(memory_space=pltpu.HBM)


def thirds(wide):
    first = wide.astype(jnp.bfloat16).astype(jnp.float32)
    second = (wide - first).astype(jnp.bfloat16).astype(jnp.float32)
    return first, second, wide - first - second


def sublanes(shape):
    return lax.broadcasted_iota(jnp.int32, shape, len(shape) - 2)


def lanes(shape):
    return lax.broadcasted_iota(jnp.int32, shape, len(shape) - 1)


def store_piece(ref, place, first, piece):
    for tile in range(piece.shape[-1] // LANES):
        ref[place, first + tile] = piece[:, tile * LANES : (tile + 1) * LANES]


def whole_block(ref, first, tiles):
    devices, _, rows, _ = ref.shape
    return jnp.concatenate(
        [ref[:, first + tile].reshape(devices * rows, LANES) for tile in range(tiles)], axis=1
    )


def scale_of(entries, half_ref, other_ref):
    total = half_ref[:1, :1] + other_ref[:1, :1]
    return jnp.minimum(1.0, math.sqrt(entries) / (jnp.sqrt(total) + 1e-06))


OWNER, HELPER, SPARE = 0, 1, 2


class Plan:
    def __init__(self, ref, blocks, devices):
        self.ref, self.blocks, self.devices = ref, blocks, devices

    @staticmethod
    def size(blocks, devices):
        return 3 * blocks + 3 * devices + 4

    def at(self, part, index):
        blocks, devices = self.blocks, self.devices
        start = {
            "slot": 0,
            "single": blocks,
            "owner": 2 * blocks,
            "load": 3 * blocks,
            "helper": 3 * blocks + devices,
            "idle": 3 * blocks + 2 * devices,
            "role": 3 * blocks + 3 * devices + 1,
            "own": 3 * blocks + 3 * devices + 2,
        }[part]
        return start + index

    def get(self, part, index=0):
        return self.ref[self.at(part, index)]

    def put(self, part, index, value):
        self.ref[self.at(part, index)] = value

    def share(self):
        return self.blocks // (self.devices - self.blocks)

    def spare_of(self, block):
        return self.get("idle", block // self.share())

    def fill(self, owner_ref, me):
        blocks, devices = self.blocks, self.devices
        spares = devices - blocks
        for device in range(devices):
            self.put("load", device, 0)
        for k in range(blocks):
            owner = owner_ref[k]
            slot = self.get("load", owner)
            self.put("owner", k, owner)
            self.put("slot", k, slot)
            self.put("load", owner, slot + 1)
        count, role = jnp.int32(0), jnp.int32(OWNER)
        for device in range(devices):
            idle = self.get("load", device) == 0
            self.put("idle", count, device)
            kind = jnp.where(count < spares, SPARE, HELPER)
            role = jnp.where(idle & (me == device), kind, role)
            count = count + idle.astype(jnp.int32)
        count = jnp.int32(spares)
        for device in range(devices):
            double = self.get("load", device) == 2
            helper = self.get("idle", jnp.minimum(count, devices - 1))
            self.put("helper", device, jnp.where(double, helper, device))
            count = count + double.astype(jnp.int32)
        for k in range(blocks):
            load = self.get("load", self.get("owner", k))
            self.put("single", k, (load == 1).astype(jnp.int32))
        self.put("role", 0, role)
        self.put("own", 0, self.get("load", me))


def pack_kernel(slots, me_ref, owner_ref, grads_ref, left_ref, right_ref, out_ref, plan_ref):
    rows_dev, rows, width = grads_ref.shape
    order = left_ref.shape[-1]
    cols = width // order
    blocks = rows_dev * cols
    tiles = order // LANES
    devices, extra = out_ref.shape[0], out_ref.shape[1] - 1
    me = me_ref[0]
    plan = Plan(plan_ref, blocks, devices)
    plan.fill(owner_ref, me)
    tile_row = sublanes((rows, LANES))
    for owner in range(devices):
        out_ref[owner, extra] = jnp.zeros((rows, LANES), jnp.bfloat16)
    row = me * rows + sublanes((rows, order))
    lower = lanes((rows, order)) <= row
    mine = lanes((rows, order)) == row
    for k in range(blocks):
        owner, slot = plan.get("owner", k), plan.get("slot", k)
        piece = grads_ref[k // cols, :, (k % cols) * order : (k % cols + 1) * order]
        store_piece(out_ref, owner, slot * tiles, piece)
        store_piece(out_ref, plan.get("helper", owner), slot * tiles, piece)
        store_piece(out_ref, plan.spare_of(k), k % plan.share() * tiles, piece)
        right = right_ref[k]
        mixed = jnp.where(lower, left_ref[k], right).astype(jnp.bfloat16)
        store_piece(out_ref, owner, (slots + slot) * tiles, mixed)
        marked = jnp.where(mine, right, 0.0)
        diagonal = marked[:, :LANES]
        for tile in range(1, tiles):
            diagonal = diagonal + marked[:, tile * LANES : (tile + 1) * LANES]
        diagonal = jnp.sum(diagonal, axis=0, keepdims=True)
        out_ref[owner, extra] = jnp.where(
            tile_row == slot, diagonal, out_ref[owner, extra].astype(jnp.float32)
        ).astype(jnp.bfloat16)


def square_kernel(grads_ref, _, __, out_ref):
    rows_dev, rows, width = grads_ref.shape
    total = jnp.zeros((8, 4 * LANES), jnp.float32)
    for i in range(rows_dev):
        for part in range(width // (4 * LANES)):
            wide = grads_ref[i, :, part * 4 * LANES : (part + 1) * 4 * LANES].astype(jnp.float32)
            wide = wide * wide
            for half in range(rows // 8):
                total = total + wide[8 * half : 8 * half + 8]
    out_ref[...] = jnp.broadcast_to(jnp.sum(total, keepdims=True), out_ref.shape)


def fifth_kernel(seed_ref, out_ref):
    order = seed_ref.shape[-1]
    for place in range(seed_ref.shape[0]):
        seed = seed_ref[place]
        high, low = split(dot(seed, seed))
        high, low = split(dot(high, high) + (dot(high, low) + dot(low, high)))
        high, low = split(-0.25 * (dot(seed, high) + dot(seed, low)))
        out_ref[place, :, :order] = high
        out_ref[place, :, order:] = low


def adam_kernel(
    order, entries, half_ref, other_ref, grads_ref, second_ref, new_ref, tile_ref
):
    rows_dev, rows, width = grads_ref.shape
    cols = width // order
    scale = scale_of(entries, half_ref, other_ref)
    sums = jnp.zeros((1, LANES), jnp.float32)
    lane = lanes((1, LANES))
    for k in range(rows_dev * cols):
        where = (k // cols, slice(None), slice((k % cols) * order, (k % cols + 1) * order))
        clipped = grads_ref[where].astype(jnp.float32) * scale
        second = 0.95 * second_ref[where] + 0.05 * clipped * clipped
        new_ref[where] = second
        step = clipped / (jnp.sqrt(second) + 1e-08)
        sums = jnp.where(lane == k, jnp.sum(step * step, keepdims=True), sums)
    tile_row = sublanes(tile_ref.shape)
    tile = jnp.zeros(tile_ref.shape, jnp.float32)
    for place, term in enumerate(thirds(sums)):
        tile = jnp.where(tile_row == place, term, tile)
    tile_ref[...] = tile.astype(jnp.bfloat16)


def owner_kernel(
    blocks,
    slots,
    entries,
    plan_ref,
    half_ref,
    other_ref,
    adam_ref,
    arrived_hbm,
    seed_hbm,
    fifth_hbm,
    roots_hbm,
    out_hbm,
    arrived_ref,
    seed_ref,
    fifth_ref,
    roots_ref,
    out_ref,
    in_sems,
    out_sems,
):
    devices, arrived_tiles, rows, lane_count = arrived_ref.shape
    order = seed_ref.shape[-1]
    tiles = order // lane_count
    plan = Plan(plan_ref, blocks, devices)
    role, load = plan.get("role"), plan.get("own")

    sources = []
    for slot in range(slots):
        sources.append((arrived_hbm, arrived_ref, (slice(None), pl.ds(slot * tiles, tiles))))
    mixed_at = (slice(None), pl.ds(slots * tiles, arrived_tiles - slots * tiles))
    sources.append((arrived_hbm, arrived_ref, mixed_at))
    for slot in range(slots):
        sources.append((fifth_hbm, fifth_ref, (slice(None), slot)))
        sources.append((seed_hbm, seed_ref, (slice(None), slot)))
    copies = [
        pltpu.make_async_copy(source.at[where], target.at[where], in_sems.at[place])
        for place, (source, target, where) in enumerate(sources)
    ]
    gradient_in, mixed_in, root_in = copies[:slots], copies[slots], copies[slots + 1 :]
    for copy in (gradient_in[0], mixed_in, *root_in[:2], *gradient_in[1:], *root_in[2:]):
        copy.start()
    shares = [
        (slice(None), pl.ds(0, tiles)),
        (slice(None), pl.ds(tiles, out_ref.shape[1] - tiles)),
    ]
    outs = [
        pltpu.make_async_copy(out_ref.at[where], out_hbm.at[where], out_sems.at[place])
        for place, where in enumerate(shares)
    ] + [
        pltpu.make_async_copy(
            roots_ref.at[:, slot], roots_hbm.at[:, slot], out_sems.at[len(shares) + slot]
        )
        for slot in range(slots)
    ]
    out_ref[:, out_ref.shape[1] - 1] = jnp.broadcast_to(
        adam_ref[...][None], (devices, rows, lane_count)
    )

    def put(first, value):
        value = value.astype(jnp.bfloat16)
        for tile in range(value.shape[1] // lane_count):
            out_ref[:, first + tile] = value[
                :, tile * lane_count : (tile + 1) * lane_count
            ].reshape(devices, rows, lane_count)

    def gradient(slot):
        return whole_block(arrived_ref, slot * tiles, tiles)

    def right_gram(block):
        return lax.dot_general(
            block, block, (((0,), (0,)), ((), ())), preferred_element_type=jnp.float32
        )

    def left_part(block, start, stop):
        return lax.dot_general(
            block,
            block[start:stop],
            (((1,), (1,)), ((), ())),
            preferred_element_type=jnp.float32,
        )

    def old_stats(slot):
        mixed = whole_block(arrived_ref, (slots + slot) * tiles, tiles)
        turned = mixed.T.astype(jnp.float32)
        mixed = mixed.astype(jnp.float32)
        row, col = sublanes((order, order)), lanes((order, order))
        diagonal = []
        tile_row = sublanes((rows, lane_count))
        for tile in range(tiles):
            total = jnp.zeros((rows, lane_count), jnp.float32)
            for source in range(tile * devices // tiles, (tile + 1) * devices // tiles):
                total = total + arrived_ref[source, arrived_tiles - 1].astype(jnp.float32)
            diagonal.append(
                jnp.sum(jnp.where(tile_row == slot, total, 0.0), axis=0, keepdims=True)
            )
        diagonal = jnp.concatenate(diagonal, axis=1)
        left_old = jnp.where(col <= row, mixed, turned)
        right_old = jnp.where(col > row, mixed, jnp.where(col == row, diagonal, turned))
        return left_old, right_old

    def work(slot):
        factor = scale_of(entries, half_ref, other_ref)
        factor = 0.05 * factor * factor
        gradient_in[slot].wait()
        block = gradient(slot)
        grams = left_part(block, 0, order), right_gram(block)
        if slot == 0:
            mixed_in.wait()
        olds = old_stats(slot)
        for copy in root_in[2 * slot : 2 * slot + 2]:
            copy.wait()
        new_pair = []
        for side, (old, gram) in enumerate(zip(olds, grams)):
            high, low = split(BETA * old + factor * gram)
            moved = dot(fifth_ref[side, slot], jnp.concatenate([high, high]))
            moved = moved + dot(fifth_ref[side, slot, :, :order], low)
            root = 1.25 * seed_ref[side, slot].astype(jnp.float32) + moved
            new_pair.append(root.astype(jnp.bfloat16))
            roots_ref[side, slot] = new_pair[-1]
        outs[len(shares) + slot].start()
        applied = dot(new_pair[0], block).astype(jnp.bfloat16)
        direction = dot(applied, new_pair[1]).astype(jnp.bfloat16).astype(jnp.float32)
        norm = jnp.sqrt(jnp.sum(direction * direction, keepdims=True)) + 1e-06
        put(slot * tiles, direction * (1.0 / norm))
        return grams

    def keep(slot):
        for copy in root_in[2 * slot : 2 * slot + 2]:
            copy.wait()
        for side in range(2):
            roots_ref[side, slot] = seed_ref[side, slot]
        outs[len(shares) + slot].start()

    @pl.when(load == 2)
    def _():
        left, _ = work(0)
        put(2 * tiles, left[:, :lane_count])
        outs[0].start()
        work(1)
        outs[1].start()

    @pl.when(load == 1)
    def _():
        left, right = work(0)
        outs[0].start()
        put(tiles, right)
        put(2 * tiles, left[:, :lane_count])
        outs[1].start()
        gradient_in[1].wait()
        keep(1)

    @pl.when(load == 0)
    def _():
        gradient_in[0].wait()
        gradient_in[1].wait()
        mixed_in.wait()

        @pl.when(role == HELPER)
        def _():
            for slot in range(slots):
                put(slot * tiles, right_gram(gradient(slot)))
            put(slots * tiles, left_part(gradient(1), 0, lane_count))

        @pl.when(role == SPARE)
        def _():
            for turn in range(3):
                put(turn * (tiles - 1), left_part(gradient(turn), lane_count, order))

        outs[0].start()
        outs[1].start()
        keep(0)
        keep(1)

    for copy in outs:
        copy.wait()


def finish_kernel(
    entries,
    plan_ref,
    half_ref,
    other_ref,
    left_ref,
    right_ref,
    back_ref,
    out_ref,
    new_left_ref,
    new_right_ref,
):
    rows_dev, rows, width = out_ref.shape
    blocks, _, order = left_ref.shape
    cols = width // order
    tiles = order // LANES
    devices, extra = back_ref.shape[0], back_ref.shape[1] - 1
    plan = Plan(plan_ref, blocks, devices)
    factor = scale_of(entries, half_ref, other_ref)
    factor = 0.05 * factor * factor
    total = jnp.zeros((rows, LANES), jnp.float32)
    for source in range(devices):
        total = total + back_ref[source, extra].astype(jnp.float32)
    norms = jnp.sqrt(jnp.sum(total, axis=0, keepdims=True))
    lane = lanes((1, LANES))
    for k in range(blocks):
        owner, slot = plan.get("owner", k), plan.get("slot", k)
        helper, single = plan.get("helper", owner), plan.get("single", k)
        spare = plan.spare_of(k)
        norm = jnp.sum(jnp.where(lane == k, norms, 0.0), axis=1, keepdims=True)
        right_from = jnp.where(single == 1, 1, slot) * tiles
        for tile in range(tiles):
            part = slice(tile * LANES, (tile + 1) * LANES)
            first = (k % cols) * order + tile * LANES
            out_ref[k // cols, :, first : first + LANES] = (
                back_ref[owner, slot * tiles + tile].astype(jnp.float32) * norm
            ).astype(jnp.bfloat16)
            if tile == 0:
                gram = back_ref[jnp.where(slot == 0, owner, helper), 2 * tiles]
            else:
                gram = back_ref[spare, k % plan.share() * (tiles - 1) + tile - 1]
            new_left_ref[k, :, part] = BETA * left_ref[k, :, part] + factor * gram.astype(
                jnp.float32
            )
            gram = back_ref[helper, right_from + tile]
            new_right_ref[k, :, part] = BETA * right_ref[k, :, part] + factor * gram.astype(
                jnp.float32
            )


def swap(values, axis, bit):
    return lax.ppermute(values, axis, [(i, i ^ bit) for i in range(lax.axis_size(axis))])


def ring_sum(values, axis, unit):
    values = values + swap(values, axis, unit)
    return values + swap(values, axis, 3 * unit)


def blk_halves(values, axis, bit):
    size, width, near, halves = lax.axis_size("blk"), lax.axis_size("zero"), 4, 2
    values = ring_sum(values, "blk", 1)
    parts = []
    for turn in range(size // near // halves):
        pairs = []
        for place in range(size):
            for group in range(width):
                upper = ((place if axis == "blk" else group) // bit) % 2
                shift = near * (turn + upper * (size // near // halves))
                source = (place + shift) % size
                pairs.append((source * width + group, place * width + group))
        parts.append(lax.ppermute(values, ("blk", "zero"), pairs))
    half = functools.reduce(jnp.add, parts)
    return half, swap(half, axis, bit)


def exchange(values):
    return lax.all_to_all(values, "blk", split_axis=0, concat_axis=0, tiled=True)


def cost(passes, order, moved):
    return pl.CostEstimate(
        flops=2 * passes * order**3, bytes_accessed=moved, transcendentals=0
    )


def local(grads, owners, left_stats, right_stats, second_moment, roots):
    devices = lax.axis_size("blk")
    rows_dev, rows, width = grads.shape
    order = left_stats.shape[-1]
    cols = width // order
    blocks = rows_dev * cols
    slots = roots.shape[2]
    tiles = order // LANES
    entries = rows_dev * lax.axis_size("zero") * order * width
    me = lax.axis_index("blk").astype(jnp.int32).reshape(1)
    owner_of = owners.reshape(blocks)
    left_old, right_old, seeds = left_stats[0], right_stats[0], roots[0]

    sent, plan = pl.pallas_call(
        functools.partial(pack_kernel, slots),
        out_shape=[
            jax.ShapeDtypeStruct((devices, 2 * slots * tiles + 1, rows, LANES), jnp.bfloat16),
            jax.ShapeDtypeStruct((Plan.size(blocks, devices),), jnp.int32),
        ],
        in_specs=[SMEM, SMEM, VMEM, VMEM, VMEM],
        out_specs=[VMEM, SMEM],
        compiler_params=grant(56),
        name="pack",
    )(me, owner_of, grads, left_old, right_old)
    arrived = exchange(sent)

    fifth = pl.pallas_call(
        fifth_kernel,
        out_shape=jax.ShapeDtypeStruct((2 * slots, order, 2 * order), jnp.bfloat16),
        in_specs=[VMEM],
        out_specs=VMEM,
        compiler_params=grant(28),
        cost_estimate=cost(12 * slots, order, 12 * slots * order * order),
        name="fifth",
    )(seeds.reshape(2 * slots, order, order))
    square = pl.pallas_call(
        square_kernel,
        out_shape=jax.ShapeDtypeStruct((8, LANES), jnp.float32),
        in_specs=[VMEM, ANY, ANY],
        out_specs=VMEM,
        compiler_params=grant(8),
        name="square",
    )(grads, fifth, sent)
    square = ring_sum(square + swap(square, "zero", 1), "zero", 2)
    square_halves = blk_halves(square, "zero", 1)

    new_second, adam = pl.pallas_call(
        functools.partial(adam_kernel, order, entries),
        out_shape=[
            jax.ShapeDtypeStruct(second_moment.shape, jnp.float32),
            jax.ShapeDtypeStruct((rows, LANES), jnp.bfloat16),
        ],
        in_specs=[VMEM, VMEM, VMEM, VMEM],
        out_specs=[VMEM, VMEM],
        compiler_params=grant(12),
        name="adam",
    )(*square_halves, grads, second_moment)

    returned_shape = (devices, 2 * tiles + 2, rows, LANES)
    fifth = fifth.reshape(2, slots, order, 2 * order)
    new_roots, returned = pl.pallas_call(
        functools.partial(owner_kernel, blocks, slots, entries),
        out_shape=[
            jax.ShapeDtypeStruct(seeds.shape, jnp.bfloat16),
            jax.ShapeDtypeStruct(returned_shape, jnp.bfloat16),
        ],
        in_specs=[SMEM, VMEM, VMEM, VMEM, HBM, HBM, HBM],
        out_specs=[HBM, HBM],
        scratch_shapes=[
            pltpu.VMEM(arrived.shape, jnp.bfloat16),
            pltpu.VMEM(seeds.shape, jnp.bfloat16),
            pltpu.VMEM(fifth.shape, jnp.bfloat16),
            pltpu.VMEM(seeds.shape, jnp.bfloat16),
            pltpu.VMEM(returned_shape, jnp.bfloat16),
            pltpu.SemaphoreType.DMA((3 * slots + 1,)),
            pltpu.SemaphoreType.DMA((slots + 2,)),
        ],
        compiler_params=grant(60),
        cost_estimate=cost(10 * slots, order, 24 * slots * order * order),
        name="owner",
    )(plan, *square_halves, adam, arrived, seeds, fifth)
    back = exchange(returned)

    placed, new_left, new_right = pl.pallas_call(
        functools.partial(finish_kernel, entries),
        out_shape=[
            jax.ShapeDtypeStruct((rows_dev, rows, width), jnp.bfloat16),
            jax.ShapeDtypeStruct(left_old.shape, jnp.float32),
            jax.ShapeDtypeStruct(right_old.shape, jnp.float32),
        ],
        in_specs=[SMEM, VMEM, VMEM, VMEM, VMEM, VMEM],
        out_specs=[VMEM, VMEM, VMEM],
        compiler_params=grant(16),
        name="finish",
    )(plan, *square_halves, left_old, right_old, back)
    return (placed, new_second, new_left[None], new_right[None], new_roots[None])


def solution(mesh):
    placed = (
        P("zero", "blk", None),
        P("zero", None, None),
        P("zero", None, "blk", None),
        P("zero", None, "blk", None),
        P("zero", "blk", None),
        P("zero", None, "blk", None, None),
    )
    return jax.shard_map(
        local,
        mesh=mesh,
        in_specs=placed,
        out_specs=(
            P("zero", "blk", None),
            P("zero", "blk", None),
            P("zero", None, "blk", None),
            P("zero", None, "blk", None),
            P("zero", None, "blk", None, None),
        ),
        check_vma=False,
    )
```

```python
import functools
import math

import jax
import jax.numpy as jnp
from jax import lax
from jax.experimental import pallas as pl
from jax.experimental.pallas import tpu as pltpu
from jax.sharding import PartitionSpec as P

BETA = 0.95
VMEM = pl.BlockSpec(memory_space=pltpu.VMEM)
SMEM = pl.BlockSpec(memory_space=pltpu.SMEM)
ANY = pl.BlockSpec(memory_space=pl.ANY)


def grant(mebibytes):
    return pltpu.CompilerParams(vmem_limit_bytes=mebibytes * 1024 * 1024)


def dot(former, latter):
    return jnp.dot(former, latter, preferred_element_type=jnp.float32)


def split(wide):
    high = wide.astype(jnp.bfloat16)
    return high, (wide - high.astype(jnp.float32)).astype(jnp.bfloat16)


LANES = 128
HBM = pl.BlockSpec(memory_space=pltpu.HBM)


def thirds(wide):
    first = wide.astype(jnp.bfloat16).astype(jnp.float32)
    second = (wide - first).astype(jnp.bfloat16).astype(jnp.float32)
    return first, second, wide - first - second


def sublanes(shape):
    return lax.broadcasted_iota(jnp.int32, shape, len(shape) - 2)


def lanes(shape):
    return lax.broadcasted_iota(jnp.int32, shape, len(shape) - 1)


def store_piece(ref, place, first, piece):
    for tile in range(piece.shape[-1] // LANES):
        ref[place, first + tile] = piece[:, tile * LANES : (tile + 1) * LANES]


def whole_block(ref, first, tiles):
    devices, _, rows, _ = ref.shape
    return jnp.concatenate(
        [ref[:, first + tile].reshape(devices * rows, LANES) for tile in range(tiles)], axis=1
    )


def scale_of(entries, half_ref, other_ref):
    total = half_ref[:1, :1] + other_ref[:1, :1]
    return jnp.minimum(1.0, math.sqrt(entries) / (jnp.sqrt(total) + 1e-06))


OWNER, HELPER, SPARE = 0, 1, 2


class Plan:
    def __init__(self, ref, blocks, devices):
        self.ref, self.blocks, self.devices = ref, blocks, devices

    @staticmethod
    def size(blocks, devices):
        return 3 * blocks + 3 * devices + 4

    def at(self, part, index):
        blocks, devices = self.blocks, self.devices
        start = {
            "slot": 0,
            "single": blocks,
            "owner": 2 * blocks,
            "load": 3 * blocks,
            "helper": 3 * blocks + devices,
            "idle": 3 * blocks + 2 * devices,
            "role": 3 * blocks + 3 * devices + 1,
            "own": 3 * blocks + 3 * devices + 2,
        }[part]
        return start + index

    def get(self, part, index=0):
        return self.ref[self.at(part, index)]

    def put(self, part, index, value):
        self.ref[self.at(part, index)] = value

    def share(self):
        return self.blocks // (self.devices - self.blocks)

    def spare_of(self, block):
        return self.get("idle", block // self.share())

    def fill(self, owner_ref, me):
        blocks, devices = self.blocks, self.devices
        spares = devices - blocks
        for device in range(devices):
            self.put("load", device, 0)
        for k in range(blocks):
            owner = owner_ref[k]
            slot = self.get("load", owner)
            self.put("owner", k, owner)
            self.put("slot", k, slot)
            self.put("load", owner, slot + 1)
        count, role = jnp.int32(0), jnp.int32(OWNER)
        for device in range(devices):
            idle = self.get("load", device) == 0
            self.put("idle", count, device)
            kind = jnp.where(count < spares, SPARE, HELPER)
            role = jnp.where(idle & (me == device), kind, role)
            count = count + idle.astype(jnp.int32)
        count = jnp.int32(spares)
        for device in range(devices):
            double = self.get("load", device) == 2
            helper = self.get("idle", jnp.minimum(count, devices - 1))
            self.put("helper", device, jnp.where(double, helper, device))
            count = count + double.astype(jnp.int32)
        for k in range(blocks):
            load = self.get("load", self.get("owner", k))
            self.put("single", k, (load == 1).astype(jnp.int32))
        self.put("role", 0, role)
        self.put("own", 0, self.get("load", me))


def pack_kernel(
    slots,
    me_ref,
    owner_ref,
    grads_hbm,
    left_hbm,
    right_hbm,
    out_hbm,
    plan_ref,
    role_ref,
    grads_ref,
    left_ref,
    right_ref,
    out_ref,
    in_sems,
    out_sems,
):
    rows_dev, rows, width = grads_ref.shape
    order = left_ref.shape[-1]
    cols = width // order
    blocks = rows_dev * cols
    tiles = order // LANES
    devices, extra = out_ref.shape[0], out_ref.shape[1] - 1
    parts = 4
    grads_in = pltpu.make_async_copy(grads_hbm, grads_ref, in_sems.at[0])
    grads_in.start()
    stats_in = []
    for part in range(parts):
        where = pl.ds(part * blocks // parts, blocks // parts)
        pair = []
        for side, (source, target) in enumerate(((left_hbm, left_ref), (right_hbm, right_ref))):
            pair.append(
                pltpu.make_async_copy(
                    source.at[where], target.at[where], in_sems.at[1 + 2 * part + side]
                )
            )
            pair[-1].start()
        stats_in.append(pair)
    me = me_ref[0]
    plan = Plan(plan_ref, blocks, devices)
    plan.fill(owner_ref, me)
    role_ref[0] = plan.get("role")
    role_ref[1] = plan.get("own")
    tile_row = sublanes((rows, LANES))
    for owner in range(devices):
        out_ref[owner, extra] = jnp.zeros((rows, LANES), jnp.bfloat16)
    grads_in.wait()
    for k in range(blocks):
        owner, slot = plan.get("owner", k), plan.get("slot", k)
        piece = grads_ref[k // cols, :, (k % cols) * order : (k % cols + 1) * order]
        store_piece(out_ref, owner, slot * tiles, piece)
        store_piece(out_ref, plan.get("helper", owner), slot * tiles, piece)
        store_piece(out_ref, plan.spare_of(k), k % plan.share() * tiles, piece)
    outs = []
    for turn, (first, count) in enumerate(
        ((0, slots * tiles), (slots * tiles, out_ref.shape[1] - slots * tiles))
    ):
        where = (slice(None), pl.ds(first, count))
        outs.append(
            pltpu.make_async_copy(out_ref.at[where], out_hbm.at[where], out_sems.at[turn])
        )
    outs[0].start()
    row = me * rows + sublanes((rows, order))
    lower = lanes((rows, order)) <= row
    mine = lanes((rows, order)) == row
    for k in range(blocks):
        if k % (blocks // parts) == 0:
            for copy in stats_in[k // (blocks // parts)]:
                copy.wait()
        owner, slot = plan.get("owner", k), plan.get("slot", k)
        right = right_ref[k]
        mixed = jnp.where(lower, left_ref[k], right).astype(jnp.bfloat16)
        store_piece(out_ref, owner, (slots + slot) * tiles, mixed)
        marked = jnp.where(mine, right, 0.0)
        diagonal = marked[:, :LANES]
        for tile in range(1, tiles):
            diagonal = diagonal + marked[:, tile * LANES : (tile + 1) * LANES]
        diagonal = jnp.sum(diagonal, axis=0, keepdims=True)
        out_ref[owner, extra] = jnp.where(
            tile_row == slot, diagonal, out_ref[owner, extra].astype(jnp.float32)
        ).astype(jnp.bfloat16)
    outs[1].start()
    for copy in outs:
        copy.wait()


def square_kernel(grads_ref, _, __, out_ref):
    rows_dev, rows, width = grads_ref.shape
    total = jnp.zeros((8, 4 * LANES), jnp.float32)
    for i in range(rows_dev):
        for part in range(width // (4 * LANES)):
            wide = grads_ref[i, :, part * 4 * LANES : (part + 1) * 4 * LANES].astype(jnp.float32)
            wide = wide * wide
            for half in range(rows // 8):
                total = total + wide[8 * half : 8 * half + 8]
    out_ref[...] = jnp.broadcast_to(jnp.sum(total, keepdims=True), out_ref.shape)


def exact_ratio(diagonal):
    rounded = diagonal.astype(jnp.bfloat16).astype(jnp.float32)
    return jnp.where(rounded == 0.0, 1.0, diagonal / jnp.where(rounded == 0.0, 1.0, rounded))


def fifth_kernel(seed_ref, out_ref, ratio_ref):
    order = seed_ref.shape[-1]
    same = sublanes((order, order)) == lanes((order, order))
    for place in range(seed_ref.shape[0]):
        seed = seed_ref[place]
        high, low = split(dot(seed, seed))
        high, low = split(dot(high, high) + (dot(high, low) + dot(low, high)))
        fifth = -0.25 * (dot(seed, high) + dot(seed, low))
        marked = jnp.where(same, fifth, 0.0)
        across = exact_ratio(jnp.sum(marked, axis=0, keepdims=True))
        down = exact_ratio(jnp.sum(marked, axis=1, keepdims=True))
        out_ref[place] = (fifth / across).astype(jnp.bfloat16)
        ratio_ref[place] = jnp.broadcast_to(down, ratio_ref.shape[1:])


def adam_work(scale, grads_ref, second_ref, new_ref, order):
    rows_dev, rows, width = grads_ref.shape
    cols = width // order
    sums = jnp.zeros((1, LANES), jnp.float32)
    lane = lanes((1, LANES))
    for k in range(rows_dev * cols):
        where = (k // cols, slice(None), slice((k % cols) * order, (k % cols + 1) * order))
        clipped = grads_ref[where].astype(jnp.float32) * scale
        second = 0.95 * second_ref[where] + 0.05 * clipped * clipped
        new_ref[where] = second
        step = clipped / (jnp.sqrt(second) + 1e-08)
        sums = jnp.where(lane == k, jnp.sum(step * step, keepdims=True), sums)
    tile_row = sublanes((rows, LANES))
    tile = jnp.zeros((rows, LANES), jnp.float32)
    for place, term in enumerate(thirds(sums)):
        tile = jnp.where(tile_row == place, term, tile)
    return tile


def owner_kernel(
    slots,
    entries,
    role_ref,
    half_ref,
    other_ref,
    grads_hbm,
    second_hbm,
    arrived_hbm,
    seed_hbm,
    fifth_hbm,
    ratio_hbm,
    roots_hbm,
    out_hbm,
    new_hbm,
    grads_ref,
    second_ref,
    arrived_ref,
    seed_ref,
    fifth_ref,
    ratio_ref,
    roots_ref,
    out_ref,
    new_ref,
    in_sems,
    out_sems,
):
    devices, arrived_tiles, rows, lane_count = arrived_ref.shape
    order = seed_ref.shape[-1]
    tiles = order // lane_count
    role, load = role_ref[0], role_ref[1]
    scale = scale_of(entries, half_ref, other_ref)
    factor = 0.05 * scale * scale

    sources = [(grads_hbm, grads_ref, ()), (second_hbm, second_ref, ())]
    sources.append((arrived_hbm, arrived_ref, (slice(None), pl.ds(0, tiles))))
    mixed_at = (slice(None), pl.ds(slots * tiles, arrived_tiles - slots * tiles))
    sources.append((arrived_hbm, arrived_ref, mixed_at))
    for slot in range(slots):
        if slot > 0:
            sources.append((arrived_hbm, arrived_ref, (slice(None), pl.ds(slot * tiles, tiles))))
        for source, target in ((fifth_hbm, fifth_ref), (ratio_hbm, ratio_ref), (seed_hbm, seed_ref)):
            sources.append((source, target, (slice(None), slot)))
    copies = [
        pltpu.make_async_copy(
            source.at[where] if where else source,
            target.at[where] if where else target,
            in_sems.at[place],
        )
        for place, (source, target, where) in enumerate(sources)
    ]
    for copy in copies:
        copy.start()
    adam_in, mixed_in = copies[:2], copies[3]
    gradient_in = [copies[2], copies[7]]
    root_in = [copies[4:7], copies[8:11]]
    shares = [
        (slice(None), pl.ds(0, tiles)),
        (slice(None), pl.ds(tiles, out_ref.shape[1] - tiles)),
    ]
    outs = [
        pltpu.make_async_copy(out_ref.at[where], out_hbm.at[where], out_sems.at[place])
        for place, where in enumerate(shares)
    ] + [
        pltpu.make_async_copy(
            roots_ref.at[:, slot], roots_hbm.at[:, slot], out_sems.at[len(shares) + slot]
        )
        for slot in range(slots)
    ] + [pltpu.make_async_copy(new_ref, new_hbm, out_sems.at[len(shares) + slots])]
    for copy in adam_in:
        copy.wait()
    adam = adam_work(scale, grads_ref, second_ref, new_ref, order)
    outs[-1].start()

    def put_sums(norms):
        tile = adam
        tile_row, lane = sublanes((rows, lane_count)), lanes((rows, lane_count))
        for slot, norm in enumerate(norms):
            for place, term in enumerate(thirds(norm)):
                tile = jnp.where((tile_row == 3 + place) & (lane == slot), term, tile)
        out_ref[:, out_ref.shape[1] - 1] = jnp.broadcast_to(
            tile.astype(jnp.bfloat16)[None], (devices, rows, lane_count)
        )

    def put(first, value):
        value = value.astype(jnp.bfloat16)
        for tile in range(value.shape[1] // lane_count):
            out_ref[:, first + tile] = value[
                :, tile * lane_count : (tile + 1) * lane_count
            ].reshape(devices, rows, lane_count)

    def gradient(slot):
        return whole_block(arrived_ref, slot * tiles, tiles)

    def right_gram(block):
        return lax.dot_general(
            block, block, (((0,), (0,)), ((), ())), preferred_element_type=jnp.float32
        )

    def left_part(block, start, stop):
        return lax.dot_general(
            block,
            block[start:stop],
            (((1,), (1,)), ((), ())),
            preferred_element_type=jnp.float32,
        )

    def old_stats(slot):
        mixed = whole_block(arrived_ref, (slots + slot) * tiles, tiles)
        turned = mixed.T.astype(jnp.float32)
        mixed = mixed.astype(jnp.float32)
        row, col = sublanes((order, order)), lanes((order, order))
        diagonal = []
        tile_row = sublanes((rows, lane_count))
        for tile in range(tiles):
            total = jnp.zeros((rows, lane_count), jnp.float32)
            for source in range(tile * devices // tiles, (tile + 1) * devices // tiles):
                total = total + arrived_ref[source, arrived_tiles - 1].astype(jnp.float32)
            diagonal.append(
                jnp.sum(jnp.where(tile_row == slot, total, 0.0), axis=0, keepdims=True)
            )
        diagonal = jnp.concatenate(diagonal, axis=1)
        left_old = jnp.where(col <= row, mixed, turned)
        right_old = jnp.where(col > row, mixed, jnp.where(col == row, diagonal, turned))
        return left_old, right_old

    def work(slot):
        gradient_in[slot].wait()
        block = gradient(slot)
        grams = left_part(block, 0, order), right_gram(block)
        if slot == 0:
            mixed_in.wait()
        olds = old_stats(slot)
        for copy in root_in[slot]:
            copy.wait()
        same = sublanes((order, order)) == lanes((order, order))
        new_pair = []
        for side, (old, gram) in enumerate(zip(olds, grams)):
            ratio = jnp.concatenate([ratio_ref[side, slot]] * tiles, axis=1)
            new = (BETA * old + factor * gram) * ratio
            across = exact_ratio(jnp.sum(jnp.where(same, new, 0.0), axis=0, keepdims=True))
            moved = dot(fifth_ref[side, slot], (new * (1.0 / across)).astype(jnp.bfloat16))
            root = 1.25 * seed_ref[side, slot].astype(jnp.float32) + moved * across
            new_pair.append(root.astype(jnp.bfloat16))
            roots_ref[side, slot] = new_pair[-1]
        outs[len(shares) + slot].start()
        applied = dot(new_pair[0], block).astype(jnp.bfloat16)
        direction = dot(applied, new_pair[1]).astype(jnp.bfloat16)
        put(slot * tiles, direction)
        wide = direction.astype(jnp.float32)
        norm = 1.0 / (jnp.sqrt(jnp.sum(wide * wide, keepdims=True)) + 1e-06)
        return grams, norm

    def keep(slot):
        for copy in root_in[slot]:
            copy.wait()
        for side in range(2):
            roots_ref[side, slot] = seed_ref[side, slot]
        outs[len(shares) + slot].start()

    @pl.when(load == 2)
    def _():
        (left, _), first = work(0)
        put(2 * tiles, left[:, :lane_count])
        outs[0].start()
        _, second = work(1)
        put_sums([first, second])
        outs[1].start()

    @pl.when(load == 1)
    def _():
        (left, right), first = work(0)
        outs[0].start()
        put(tiles, right)
        put(2 * tiles, left[:, :lane_count])
        put_sums([first])
        outs[1].start()
        gradient_in[1].wait()
        keep(1)

    @pl.when(load == 0)
    def _():
        gradient_in[0].wait()
        gradient_in[1].wait()
        mixed_in.wait()
        put_sums([])

        @pl.when(role == HELPER)
        def _():
            for slot in range(slots):
                put(slot * tiles, right_gram(gradient(slot)))
            put(slots * tiles, left_part(gradient(1), 0, lane_count))

        @pl.when(role == SPARE)
        def _():
            for turn in range(3):
                put(turn * (tiles - 1), left_part(gradient(turn), lane_count, order))

        outs[0].start()
        outs[1].start()
        keep(0)
        keep(1)

    for copy in outs:
        copy.wait()


def finish_kernel(
    entries,
    plan_ref,
    half_ref,
    other_ref,
    left_ref,
    right_ref,
    back_ref,
    out_ref,
    new_left_ref,
    new_right_ref,
):
    rows_dev, rows, width = out_ref.shape
    blocks, _, order = left_ref.shape
    cols = width // order
    tiles = order // LANES
    devices, extra = back_ref.shape[0], back_ref.shape[1] - 1
    plan = Plan(plan_ref, blocks, devices)
    factor = scale_of(entries, half_ref, other_ref)
    factor = 0.05 * factor * factor
    total = jnp.zeros((rows, LANES), jnp.float32)
    for source in range(devices):
        total = total + back_ref[source, extra].astype(jnp.float32)
    tile_row, lane = sublanes((rows, LANES)), lanes((rows, LANES))
    norms = jnp.sqrt(jnp.sum(jnp.where(tile_row < 3, total, 0.0), axis=0, keepdims=True))
    for k in range(blocks):
        owner, slot = plan.get("owner", k), plan.get("slot", k)
        helper, single = plan.get("helper", owner), plan.get("single", k)
        spare = plan.spare_of(k)
        norm = jnp.sum(jnp.where(lane[:1] == k, norms, 0.0), axis=1, keepdims=True)
        inverse = jnp.where(
            (lane == slot) & (tile_row >= 3) & (tile_row < 6),
            back_ref[owner, extra].astype(jnp.float32),
            0.0,
        )
        norm = norm * jnp.sum(inverse, keepdims=True)
        right_from = jnp.where(single == 1, 1, slot) * tiles
        for tile in range(tiles):
            part = slice(tile * LANES, (tile + 1) * LANES)
            first = (k % cols) * order + tile * LANES
            out_ref[k // cols, :, first : first + LANES] = (
                back_ref[owner, slot * tiles + tile].astype(jnp.float32) * norm
            ).astype(jnp.bfloat16)
            if tile == 0:
                gram = back_ref[jnp.where(slot == 0, owner, helper), 2 * tiles]
            else:
                gram = back_ref[spare, k % plan.share() * (tiles - 1) + tile - 1]
            new_left_ref[k, :, part] = BETA * left_ref[k, :, part] + factor * gram.astype(
                jnp.float32
            )
            gram = back_ref[helper, right_from + tile]
            new_right_ref[k, :, part] = BETA * right_ref[k, :, part] + factor * gram.astype(
                jnp.float32
            )


def swap(values, axis, bit):
    return lax.ppermute(values, axis, [(i, i ^ bit) for i in range(lax.axis_size(axis))])


def ring_sum(values, axis, unit):
    values = values + swap(values, axis, unit)
    return values + swap(values, axis, 3 * unit)


def blk_halves(values, axis, bit):
    size, width, near, halves = lax.axis_size("blk"), lax.axis_size("zero"), 4, 2
    values = ring_sum(values, "blk", 1)
    parts = []
    for turn in range(size // near // halves):
        pairs = []
        for place in range(size):
            for group in range(width):
                upper = ((place if axis == "blk" else group) // bit) % 2
                shift = near * (turn + upper * (size // near // halves))
                source = (place + shift) % size
                pairs.append((source * width + group, place * width + group))
        parts.append(lax.ppermute(values, ("blk", "zero"), pairs))
    half = functools.reduce(jnp.add, parts)
    return half, swap(half, axis, bit)


def exchange(values):
    return lax.all_to_all(values, "blk", split_axis=0, concat_axis=0, tiled=True)


def cost(passes, order, moved):
    return pl.CostEstimate(
        flops=2 * passes * order**3, bytes_accessed=moved, transcendentals=0
    )


def local(grads, owners, left_stats, right_stats, second_moment, roots):
    devices = lax.axis_size("blk")
    rows_dev, rows, width = grads.shape
    order = left_stats.shape[-1]
    cols = width // order
    blocks = rows_dev * cols
    slots = roots.shape[2]
    tiles = order // LANES
    entries = rows_dev * lax.axis_size("zero") * order * width
    me = lax.axis_index("blk").astype(jnp.int32).reshape(1)
    owner_of = owners.reshape(blocks)
    left_old, right_old, seeds = left_stats[0], right_stats[0], roots[0]

    sent_shape = (devices, 2 * slots * tiles + 1, rows, LANES)
    sent, plan, role = pl.pallas_call(
        functools.partial(pack_kernel, slots),
        out_shape=[
            jax.ShapeDtypeStruct(sent_shape, jnp.bfloat16),
            jax.ShapeDtypeStruct((Plan.size(blocks, devices),), jnp.int32),
            jax.ShapeDtypeStruct((2,), jnp.int32),
        ],
        in_specs=[SMEM, SMEM, HBM, HBM, HBM],
        out_specs=[HBM, SMEM, SMEM],
        scratch_shapes=[
            pltpu.VMEM(grads.shape, jnp.bfloat16),
            pltpu.VMEM(left_old.shape, jnp.float32),
            pltpu.VMEM(right_old.shape, jnp.float32),
            pltpu.VMEM(sent_shape, jnp.bfloat16),
            pltpu.SemaphoreType.DMA((9,)),
            pltpu.SemaphoreType.DMA((2,)),
        ],
        compiler_params=grant(60),
        name="pack",
    )(me, owner_of, grads, left_old, right_old)
    arrived = exchange(sent)

    fifth, ratio = pl.pallas_call(
        fifth_kernel,
        out_shape=[
            jax.ShapeDtypeStruct((2 * slots, order, order), jnp.bfloat16),
            jax.ShapeDtypeStruct((2 * slots, order, LANES), jnp.float32),
        ],
        in_specs=[VMEM],
        out_specs=[VMEM, VMEM],
        compiler_params=grant(28),
        cost_estimate=cost(12 * slots, order, 12 * slots * order * order),
        name="fifth",
    )(seeds.reshape(2 * slots, order, order))
    square = pl.pallas_call(
        square_kernel,
        out_shape=jax.ShapeDtypeStruct((8, LANES), jnp.float32),
        in_specs=[VMEM, ANY, ANY],
        out_specs=VMEM,
        compiler_params=grant(8),
        name="square",
    )(grads, fifth, sent)
    square = ring_sum(square + swap(square, "zero", 1), "zero", 2)
    square_halves = blk_halves(square, "zero", 1)

    returned_shape = (devices, 2 * tiles + 2, rows, LANES)
    fifth = fifth.reshape(2, slots, order, order)
    ratio = ratio.reshape(2, slots, order, LANES)
    new_roots, returned, new_second = pl.pallas_call(
        functools.partial(owner_kernel, slots, entries),
        out_shape=[
            jax.ShapeDtypeStruct(seeds.shape, jnp.bfloat16),
            jax.ShapeDtypeStruct(returned_shape, jnp.bfloat16),
            jax.ShapeDtypeStruct(second_moment.shape, jnp.float32),
        ],
        in_specs=[SMEM, VMEM, VMEM, HBM, HBM, HBM, HBM, HBM, HBM],
        out_specs=[HBM, HBM, HBM],
        scratch_shapes=[
            pltpu.VMEM(grads.shape, jnp.bfloat16),
            pltpu.VMEM(second_moment.shape, jnp.float32),
            pltpu.VMEM(arrived.shape, jnp.bfloat16),
            pltpu.VMEM(seeds.shape, jnp.bfloat16),
            pltpu.VMEM(fifth.shape, jnp.bfloat16),
            pltpu.VMEM(ratio.shape, jnp.float32),
            pltpu.VMEM(seeds.shape, jnp.bfloat16),
            pltpu.VMEM(returned_shape, jnp.bfloat16),
            pltpu.VMEM(second_moment.shape, jnp.float32),
            pltpu.SemaphoreType.DMA((4 * slots + 3,)),
            pltpu.SemaphoreType.DMA((slots + 3,)),
        ],
        compiler_params=grant(60),
        cost_estimate=cost(8 * slots, order, 24 * slots * order * order),
        name="owner",
    )(role, *square_halves, grads, second_moment, arrived, seeds, fifth, ratio)
    back = exchange(returned)

    placed, new_left, new_right = pl.pallas_call(
        functools.partial(finish_kernel, entries),
        out_shape=[
            jax.ShapeDtypeStruct((rows_dev, rows, width), jnp.bfloat16),
            jax.ShapeDtypeStruct(left_old.shape, jnp.float32),
            jax.ShapeDtypeStruct(right_old.shape, jnp.float32),
        ],
        in_specs=[SMEM, VMEM, VMEM, VMEM, VMEM, VMEM],
        out_specs=[VMEM, VMEM, VMEM],
        compiler_params=grant(16),
        name="finish",
    )(plan, *square_halves, left_old, right_old, back)
    return (placed, new_second, new_left[None], new_right[None], new_roots[None])


def solution(mesh):
    placed = (
        P("zero", "blk", None),
        P("zero", None, None),
        P("zero", None, "blk", None),
        P("zero", None, "blk", None),
        P("zero", "blk", None),
        P("zero", None, "blk", None, None),
    )
    return jax.shard_map(
        local,
        mesh=mesh,
        in_specs=placed,
        out_specs=(
            P("zero", "blk", None),
            P("zero", "blk", None),
            P("zero", None, "blk", None),
            P("zero", None, "blk", None),
            P("zero", None, "blk", None, None),
        ),
        check_vma=False,
    )
```

```python
import functools
import math

import jax
import jax.numpy as jnp
from jax import lax
from jax.experimental import pallas as pl
from jax.experimental.pallas import tpu as pltpu
from jax.sharding import PartitionSpec as P

BETA = 0.95
VMEM = pl.BlockSpec(memory_space=pltpu.VMEM)
SMEM = pl.BlockSpec(memory_space=pltpu.SMEM)
ANY = pl.BlockSpec(memory_space=pl.ANY)


def grant(mebibytes):
    return pltpu.CompilerParams(vmem_limit_bytes=mebibytes * 1024 * 1024)


def dot(former, latter):
    return jnp.dot(former, latter, preferred_element_type=jnp.float32)


def split(wide):
    high = wide.astype(jnp.bfloat16)
    return high, (wide - high.astype(jnp.float32)).astype(jnp.bfloat16)


LANES = 128
ROWS = 16
EXTRA = 8
HBM = pl.BlockSpec(memory_space=pltpu.HBM)


def thirds(wide):
    first = wide.astype(jnp.bfloat16).astype(jnp.float32)
    second = (wide - first).astype(jnp.bfloat16).astype(jnp.float32)
    return first, second, wide - first - second


def sublanes(shape):
    return lax.broadcasted_iota(jnp.int32, shape, len(shape) - 2)


def lanes(shape):
    return lax.broadcasted_iota(jnp.int32, shape, len(shape) - 1)


def span(tile):
    if isinstance(tile, int):
        return pl.ds(tile * ROWS, ROWS)
    return pl.ds(pl.multiple_of(tile * ROWS, ROWS), ROWS)


def store_piece(ref, place, first, piece):
    for tile in range(piece.shape[-1] // LANES):
        ref[place, span(first + tile)] = piece[:, tile * LANES : (tile + 1) * LANES]


def whole_block(ref, first, tiles):
    return jnp.concatenate(
        [ref[:, span(first + tile)].reshape(-1, LANES) for tile in range(tiles)], axis=1
    )


def scale_of(entries, half_ref, other_ref):
    total = half_ref[:1, :1] + other_ref[:1, :1]
    return jnp.minimum(1.0, math.sqrt(entries) / (jnp.sqrt(total) + 1e-06))


OWNER, HELPER, SPARE = 0, 1, 2


class Plan:
    def __init__(self, ref, blocks, devices):
        self.ref, self.blocks, self.devices = ref, blocks, devices

    @staticmethod
    def size(blocks, devices):
        return 3 * blocks + 3 * devices + 4

    def at(self, part, index):
        blocks, devices = self.blocks, self.devices
        start = {
            "slot": 0,
            "single": blocks,
            "owner": 2 * blocks,
            "load": 3 * blocks,
            "helper": 3 * blocks + devices,
            "idle": 3 * blocks + 2 * devices,
            "role": 3 * blocks + 3 * devices + 1,
            "own": 3 * blocks + 3 * devices + 2,
        }[part]
        return start + index

    def get(self, part, index=0):
        return self.ref[self.at(part, index)]

    def put(self, part, index, value):
        self.ref[self.at(part, index)] = value

    def share(self):
        return self.blocks // (self.devices - self.blocks)

    def spare_of(self, block):
        return self.get("idle", block // self.share())

    def fill(self, owner_ref, me):
        blocks, devices = self.blocks, self.devices
        spares = devices - blocks
        for device in range(devices):
            self.put("load", device, 0)
        for k in range(blocks):
            owner = owner_ref[k]
            slot = self.get("load", owner)
            self.put("owner", k, owner)
            self.put("slot", k, slot)
            self.put("load", owner, slot + 1)
        count, role = jnp.int32(0), jnp.int32(OWNER)
        for device in range(devices):
            idle = self.get("load", device) == 0
            self.put("idle", count, device)
            kind = jnp.where(count < spares, SPARE, HELPER)
            role = jnp.where(idle & (me == device), kind, role)
            count = count + idle.astype(jnp.int32)
        count = jnp.int32(spares)
        for device in range(devices):
            double = self.get("load", device) == 2
            helper = self.get("idle", jnp.minimum(count, devices - 1))
            self.put("helper", device, jnp.where(double, helper, device))
            count = count + double.astype(jnp.int32)
        for k in range(blocks):
            load = self.get("load", self.get("owner", k))
            self.put("single", k, (load == 1).astype(jnp.int32))
        self.put("role", 0, role)
        self.put("own", 0, self.get("load", me))


def pack_kernel(
    slots,
    me_ref,
    owner_ref,
    grads_hbm,
    left_hbm,
    right_hbm,
    out_hbm,
    plan_ref,
    role_ref,
    grads_ref,
    left_ref,
    right_ref,
    out_ref,
    in_sems,
    out_sems,
):
    rows_dev, rows, width = grads_ref.shape
    order = left_ref.shape[-1]
    cols = width // order
    blocks = rows_dev * cols
    tiles = order // LANES
    devices, extra = out_ref.shape[0], pl.ds(out_ref.shape[1] - EXTRA, EXTRA)
    parts = 4
    grads_in = pltpu.make_async_copy(grads_hbm, grads_ref, in_sems.at[0])
    grads_in.start()
    stats_in = []
    for part in range(parts):
        where = pl.ds(part * blocks // parts, blocks // parts)
        pair = []
        for side, (source, target) in enumerate(((left_hbm, left_ref), (right_hbm, right_ref))):
            pair.append(
                pltpu.make_async_copy(
                    source.at[where], target.at[where], in_sems.at[1 + 2 * part + side]
                )
            )
            pair[-1].start()
        stats_in.append(pair)
    me = me_ref[0]
    plan = Plan(plan_ref, blocks, devices)
    plan.fill(owner_ref, me)
    role_ref[0] = plan.get("role")
    role_ref[1] = plan.get("own")
    tile_row = sublanes((EXTRA, LANES))
    for owner in range(devices):
        out_ref[owner, extra] = jnp.zeros((EXTRA, LANES), jnp.bfloat16)
    grads_in.wait()
    for k in range(blocks):
        owner, slot = plan.get("owner", k), plan.get("slot", k)
        piece = grads_ref[k // cols, :, (k % cols) * order : (k % cols + 1) * order]
        store_piece(out_ref, owner, slot * tiles, piece)
        store_piece(out_ref, plan.get("helper", owner), slot * tiles, piece)
        store_piece(out_ref, plan.spare_of(k), k % plan.share() * tiles, piece)
    outs = []
    for turn, (first, count) in enumerate(
        (
            (0, slots * tiles * rows),
            (slots * tiles * rows, out_ref.shape[1] - slots * tiles * rows),
        )
    ):
        where = (slice(None), pl.ds(first, count))
        outs.append(
            pltpu.make_async_copy(out_ref.at[where], out_hbm.at[where], out_sems.at[turn])
        )
    outs[0].start()
    row = me * rows + sublanes((rows, order))
    lower = lanes((rows, order)) <= row
    mine = lanes((rows, order)) == row
    for k in range(blocks):
        if k % (blocks // parts) == 0:
            for copy in stats_in[k // (blocks // parts)]:
                copy.wait()
        owner, slot = plan.get("owner", k), plan.get("slot", k)
        right = right_ref[k]
        mixed = jnp.where(lower, left_ref[k], right).astype(jnp.bfloat16)
        store_piece(out_ref, owner, (slots + slot) * tiles, mixed)
        marked = jnp.where(mine, right, 0.0)
        diagonal = marked[:, :LANES]
        for tile in range(1, tiles):
            diagonal = diagonal + marked[:, tile * LANES : (tile + 1) * LANES]
        diagonal = jnp.sum(diagonal, axis=0, keepdims=True)
        out_ref[owner, extra] = jnp.where(
            tile_row == slot, diagonal, out_ref[owner, extra].astype(jnp.float32)
        ).astype(jnp.bfloat16)
    outs[1].start()
    for copy in outs:
        copy.wait()


def square_kernel(grads_ref, _, __, out_ref):
    rows_dev, rows, width = grads_ref.shape
    total = jnp.zeros((8, 4 * LANES), jnp.float32)
    for i in range(rows_dev):
        for part in range(width // (4 * LANES)):
            wide = grads_ref[i, :, part * 4 * LANES : (part + 1) * 4 * LANES].astype(jnp.float32)
            wide = wide * wide
            for half in range(rows // 8):
                total = total + wide[8 * half : 8 * half + 8]
    out_ref[...] = jnp.broadcast_to(jnp.sum(total, keepdims=True), out_ref.shape)


def exact_ratio(diagonal):
    rounded = diagonal.astype(jnp.bfloat16).astype(jnp.float32)
    return jnp.where(rounded == 0.0, 1.0, diagonal / jnp.where(rounded == 0.0, 1.0, rounded))


def fifth_kernel(seed_ref, out_ref, ratio_ref):
    order = seed_ref.shape[-1]
    same = sublanes((order, order)) == lanes((order, order))
    for place in range(seed_ref.shape[0]):
        seed = seed_ref[place]
        high, low = split(dot(seed, seed))
        high, low = split(dot(high, high) + (dot(high, low) + dot(low, high)))
        fifth = -0.25 * (dot(seed, high) + dot(seed, low))
        marked = jnp.where(same, fifth, 0.0)
        across = exact_ratio(jnp.sum(marked, axis=0, keepdims=True))
        down = exact_ratio(jnp.sum(marked, axis=1, keepdims=True))
        out_ref[place] = (fifth / across).astype(jnp.bfloat16)
        ratio_ref[place] = jnp.broadcast_to(down, ratio_ref.shape[1:])


def adam_work(scale, grads_ref, second_ref, new_ref, order):
    rows_dev, rows, width = grads_ref.shape
    cols = width // order
    sums = jnp.zeros((1, LANES), jnp.float32)
    lane = lanes((1, LANES))
    for k in range(rows_dev * cols):
        where = (k // cols, slice(None), slice((k % cols) * order, (k % cols + 1) * order))
        clipped = grads_ref[where].astype(jnp.float32) * scale
        second = 0.95 * second_ref[where] + 0.05 * clipped * clipped
        new_ref[where] = second
        step = clipped / (jnp.sqrt(second) + 1e-08)
        sums = jnp.where(lane == k, jnp.sum(step * step, keepdims=True), sums)
    tile_row = sublanes((EXTRA, LANES))
    tile = jnp.zeros((EXTRA, LANES), jnp.float32)
    for place, term in enumerate(thirds(sums)):
        tile = jnp.where(tile_row == place, term, tile)
    return tile


def owner_kernel(
    slots,
    entries,
    role_ref,
    half_ref,
    other_ref,
    grads_hbm,
    second_hbm,
    arrived_hbm,
    seed_hbm,
    fifth_hbm,
    ratio_hbm,
    roots_hbm,
    out_hbm,
    new_hbm,
    grads_ref,
    second_ref,
    arrived_ref,
    seed_ref,
    fifth_ref,
    ratio_ref,
    roots_ref,
    out_ref,
    new_ref,
    in_sems,
    out_sems,
):
    devices, arrived_rows, lane_count = arrived_ref.shape
    order = seed_ref.shape[-1]
    tiles = order // lane_count
    piece = tiles * ROWS
    role, load = role_ref[0], role_ref[1]
    scale = scale_of(entries, half_ref, other_ref)
    factor = 0.05 * scale * scale

    sources = [(grads_hbm, grads_ref, ()), (second_hbm, second_ref, ())]
    sources.append((arrived_hbm, arrived_ref, (slice(None), pl.ds(0, piece))))
    mixed_at = (slice(None), pl.ds(slots * piece, arrived_rows - slots * piece))
    sources.append((arrived_hbm, arrived_ref, mixed_at))
    for slot in range(slots):
        if slot > 0:
            sources.append((arrived_hbm, arrived_ref, (slice(None), pl.ds(slot * piece, piece))))
        for source, target in ((fifth_hbm, fifth_ref), (ratio_hbm, ratio_ref), (seed_hbm, seed_ref)):
            sources.append((source, target, (slice(None), slot)))
    copies = [
        pltpu.make_async_copy(
            source.at[where] if where else source,
            target.at[where] if where else target,
            in_sems.at[place],
        )
        for place, (source, target, where) in enumerate(sources)
    ]
    for copy in copies:
        copy.start()
    adam_in, mixed_in = copies[:2], copies[3]
    gradient_in = [copies[2], copies[7]]
    root_in = [copies[4:7], copies[8:11]]
    shares = [
        (slice(None), pl.ds(0, piece)),
        (slice(None), pl.ds(piece, out_ref.shape[1] - piece)),
    ]
    outs = [
        pltpu.make_async_copy(out_ref.at[where], out_hbm.at[where], out_sems.at[place])
        for place, where in enumerate(shares)
    ] + [
        pltpu.make_async_copy(
            roots_ref.at[:, slot], roots_hbm.at[:, slot], out_sems.at[len(shares) + slot]
        )
        for slot in range(slots)
    ] + [pltpu.make_async_copy(new_ref, new_hbm, out_sems.at[len(shares) + slots])]
    for copy in adam_in:
        copy.wait()
    adam = adam_work(scale, grads_ref, second_ref, new_ref, order)
    outs[-1].start()

    def put_sums(norms):
        tile = adam
        tile_row, lane = sublanes((EXTRA, lane_count)), lanes((EXTRA, lane_count))
        for slot, norm in enumerate(norms):
            for place, term in enumerate(thirds(norm)):
                tile = jnp.where((tile_row == 3 + place) & (lane == slot), term, tile)
        out_ref[:, pl.ds(out_ref.shape[1] - EXTRA, EXTRA)] = jnp.broadcast_to(
            tile.astype(jnp.bfloat16)[None], (devices, EXTRA, lane_count)
        )

    def put(first, value):
        value = value.astype(jnp.bfloat16)
        for tile in range(value.shape[1] // lane_count):
            out_ref[:, span(first + tile)] = value[
                :, tile * lane_count : (tile + 1) * lane_count
            ].reshape(devices, ROWS, lane_count)

    def gradient(slot):
        return whole_block(arrived_ref, slot * tiles, tiles)

    def right_gram(block):
        return lax.dot_general(
            block, block, (((0,), (0,)), ((), ())), preferred_element_type=jnp.float32
        )

    def left_part(block, start, stop):
        return lax.dot_general(
            block,
            block[start:stop],
            (((1,), (1,)), ((), ())),
            preferred_element_type=jnp.float32,
        )

    def old_stats(slot):
        mixed = whole_block(arrived_ref, (slots + slot) * tiles, tiles)
        turned = mixed.T.astype(jnp.float32)
        mixed = mixed.astype(jnp.float32)
        row, col = sublanes((order, order)), lanes((order, order))
        diagonal = []
        tile_row = sublanes((EXTRA, lane_count))
        for tile in range(tiles):
            total = jnp.zeros((EXTRA, lane_count), jnp.float32)
            for source in range(tile * devices // tiles, (tile + 1) * devices // tiles):
                total = total + arrived_ref[source, pl.ds(arrived_rows - EXTRA, EXTRA)].astype(
                    jnp.float32
                )
            diagonal.append(
                jnp.sum(jnp.where(tile_row == slot, total, 0.0), axis=0, keepdims=True)
            )
        diagonal = jnp.concatenate(diagonal, axis=1)
        left_old = jnp.where(col <= row, mixed, turned)
        right_old = jnp.where(col > row, mixed, jnp.where(col == row, diagonal, turned))
        return left_old, right_old

    def work(slot):
        gradient_in[slot].wait()
        block = gradient(slot)
        grams = left_part(block, 0, order), right_gram(block)
        if slot == 0:
            mixed_in.wait()
        olds = old_stats(slot)
        for copy in root_in[slot]:
            copy.wait()
        same = sublanes((order, order)) == lanes((order, order))
        new_pair = []
        for side, (old, gram) in enumerate(zip(olds, grams)):
            ratio = jnp.concatenate([ratio_ref[side, slot]] * tiles, axis=1)
            new = (BETA * old + factor * gram) * ratio
            across = exact_ratio(jnp.sum(jnp.where(same, new, 0.0), axis=0, keepdims=True))
            moved = dot(fifth_ref[side, slot], (new * (1.0 / across)).astype(jnp.bfloat16))
            root = 1.25 * seed_ref[side, slot].astype(jnp.float32) + moved * across
            new_pair.append(root.astype(jnp.bfloat16))
            roots_ref[side, slot] = new_pair[-1]
        outs[len(shares) + slot].start()
        applied = dot(new_pair[0], block).astype(jnp.bfloat16)
        direction = dot(applied, new_pair[1]).astype(jnp.bfloat16)
        put(slot * tiles, direction)
        wide = direction.astype(jnp.float32)
        norm = 1.0 / (jnp.sqrt(jnp.sum(wide * wide, keepdims=True)) + 1e-06)
        return grams, norm

    def keep(slot):
        for copy in root_in[slot]:
            copy.wait()
        for side in range(2):
            roots_ref[side, slot] = seed_ref[side, slot]
        outs[len(shares) + slot].start()

    @pl.when(load == 2)
    def _():
        (left, _), first = work(0)
        put(2 * tiles, left[:, :lane_count])
        outs[0].start()
        _, second = work(1)
        put_sums([first, second])
        outs[1].start()

    @pl.when(load == 1)
    def _():
        (left, right), first = work(0)
        outs[0].start()
        put(tiles, right)
        put(2 * tiles, left[:, :lane_count])
        put_sums([first])
        outs[1].start()
        gradient_in[1].wait()
        keep(1)

    @pl.when(load == 0)
    def _():
        gradient_in[0].wait()
        gradient_in[1].wait()
        mixed_in.wait()
        put_sums([])

        @pl.when(role == HELPER)
        def _():
            for slot in range(slots):
                put(slot * tiles, right_gram(gradient(slot)))
            put(slots * tiles, left_part(gradient(1), 0, lane_count))

        @pl.when(role == SPARE)
        def _():
            for turn in range(3):
                put(turn * (tiles - 1), left_part(gradient(turn), lane_count, order))

        outs[0].start()
        outs[1].start()
        keep(0)
        keep(1)

    for copy in outs:
        copy.wait()


def finish_kernel(
    entries,
    plan_ref,
    half_ref,
    other_ref,
    left_ref,
    right_ref,
    back_ref,
    out_ref,
    new_left_ref,
    new_right_ref,
):
    rows_dev, rows, width = out_ref.shape
    blocks, _, order = left_ref.shape
    cols = width // order
    tiles = order // LANES
    devices, extra = back_ref.shape[0], pl.ds(back_ref.shape[1] - EXTRA, EXTRA)
    plan = Plan(plan_ref, blocks, devices)
    factor = scale_of(entries, half_ref, other_ref)
    factor = 0.05 * factor * factor
    total = jnp.zeros((EXTRA, LANES), jnp.float32)
    for source in range(devices):
        total = total + back_ref[source, extra].astype(jnp.float32)
    tile_row, lane = sublanes((EXTRA, LANES)), lanes((EXTRA, LANES))
    norms = jnp.sqrt(jnp.sum(jnp.where(tile_row < 3, total, 0.0), axis=0, keepdims=True))
    for k in range(blocks):
        owner, slot = plan.get("owner", k), plan.get("slot", k)
        helper, single = plan.get("helper", owner), plan.get("single", k)
        spare = plan.spare_of(k)
        norm = jnp.sum(jnp.where(lane[:1] == k, norms, 0.0), axis=1, keepdims=True)
        inverse = jnp.where(
            (lane == slot) & (tile_row >= 3) & (tile_row < 6),
            back_ref[owner, extra].astype(jnp.float32),
            0.0,
        )
        norm = norm * jnp.sum(inverse, keepdims=True)
        right_from = jnp.where(single == 1, 1, slot) * tiles
        for tile in range(tiles):
            part = slice(tile * LANES, (tile + 1) * LANES)
            first = (k % cols) * order + tile * LANES
            out_ref[k // cols, :, first : first + LANES] = (
                back_ref[owner, span(slot * tiles + tile)].astype(jnp.float32) * norm
            ).astype(jnp.bfloat16)
            if tile == 0:
                gram = back_ref[jnp.where(slot == 0, owner, helper), span(2 * tiles)]
            else:
                gram = back_ref[spare, span(k % plan.share() * (tiles - 1) + tile - 1)]
            new_left_ref[k, :, part] = BETA * left_ref[k, :, part] + factor * gram.astype(
                jnp.float32
            )
            gram = back_ref[helper, span(right_from + tile)]
            new_right_ref[k, :, part] = BETA * right_ref[k, :, part] + factor * gram.astype(
                jnp.float32
            )


def swap(values, axis, bit):
    return lax.ppermute(values, axis, [(i, i ^ bit) for i in range(lax.axis_size(axis))])


def ring_sum(values, axis, unit):
    values = values + swap(values, axis, unit)
    return values + swap(values, axis, 3 * unit)


def blk_halves(values, axis, bit):
    size, width, near, halves = lax.axis_size("blk"), lax.axis_size("zero"), 4, 2
    values = ring_sum(values, "blk", 1)
    parts = []
    for turn in range(size // near // halves):
        pairs = []
        for place in range(size):
            for group in range(width):
                upper = ((place if axis == "blk" else group) // bit) % 2
                shift = near * (turn + upper * (size // near // halves))
                source = (place + shift) % size
                pairs.append((source * width + group, place * width + group))
        parts.append(lax.ppermute(values, ("blk", "zero"), pairs))
    half = functools.reduce(jnp.add, parts)
    return half, swap(half, axis, bit)


def exchange(values):
    return lax.all_to_all(values, "blk", split_axis=0, concat_axis=0, tiled=True)


def cost(passes, order, moved):
    return pl.CostEstimate(
        flops=2 * passes * order**3, bytes_accessed=moved, transcendentals=0
    )


def local(grads, owners, left_stats, right_stats, second_moment, roots):
    devices = lax.axis_size("blk")
    rows_dev, rows, width = grads.shape
    order = left_stats.shape[-1]
    cols = width // order
    blocks = rows_dev * cols
    slots = roots.shape[2]
    tiles = order // LANES
    entries = rows_dev * lax.axis_size("zero") * order * width
    me = lax.axis_index("blk").astype(jnp.int32).reshape(1)
    owner_of = owners.reshape(blocks)
    left_old, right_old, seeds = left_stats[0], right_stats[0], roots[0]

    sent_shape = (devices, 2 * slots * tiles * rows + EXTRA, LANES)
    sent, plan, role = pl.pallas_call(
        functools.partial(pack_kernel, slots),
        out_shape=[
            jax.ShapeDtypeStruct(sent_shape, jnp.bfloat16),
            jax.ShapeDtypeStruct((Plan.size(blocks, devices),), jnp.int32),
            jax.ShapeDtypeStruct((2,), jnp.int32),
        ],
        in_specs=[SMEM, SMEM, HBM, HBM, HBM],
        out_specs=[HBM, SMEM, SMEM],
        scratch_shapes=[
            pltpu.VMEM(grads.shape, jnp.bfloat16),
            pltpu.VMEM(left_old.shape, jnp.float32),
            pltpu.VMEM(right_old.shape, jnp.float32),
            pltpu.VMEM(sent_shape, jnp.bfloat16),
            pltpu.SemaphoreType.DMA((9,)),
            pltpu.SemaphoreType.DMA((2,)),
        ],
        compiler_params=grant(60),
        name="pack",
    )(me, owner_of, grads, left_old, right_old)
    arrived = exchange(sent)

    fifth, ratio = pl.pallas_call(
        fifth_kernel,
        out_shape=[
            jax.ShapeDtypeStruct((2 * slots, order, order), jnp.bfloat16),
            jax.ShapeDtypeStruct((2 * slots, order, LANES), jnp.float32),
        ],
        in_specs=[VMEM],
        out_specs=[VMEM, VMEM],
        compiler_params=grant(28),
        cost_estimate=cost(12 * slots, order, 12 * slots * order * order),
        name="fifth",
    )(seeds.reshape(2 * slots, order, order))
    square = pl.pallas_call(
        square_kernel,
        out_shape=jax.ShapeDtypeStruct((8, LANES), jnp.float32),
        in_specs=[VMEM, ANY, ANY],
        out_specs=VMEM,
        compiler_params=grant(8),
        name="square",
    )(grads, fifth, sent)
    square = ring_sum(square + swap(square, "zero", 1), "zero", 2)
    square_halves = blk_halves(square, "zero", 1)

    returned_shape = (devices, (2 * tiles + 1) * rows + EXTRA, LANES)
    fifth = fifth.reshape(2, slots, order, order)
    ratio = ratio.reshape(2, slots, order, LANES)
    new_roots, returned, new_second = pl.pallas_call(
        functools.partial(owner_kernel, slots, entries),
        out_shape=[
            jax.ShapeDtypeStruct(seeds.shape, jnp.bfloat16),
            jax.ShapeDtypeStruct(returned_shape, jnp.bfloat16),
            jax.ShapeDtypeStruct(second_moment.shape, jnp.float32),
        ],
        in_specs=[SMEM, VMEM, VMEM, HBM, HBM, HBM, HBM, HBM, HBM],
        out_specs=[HBM, HBM, HBM],
        scratch_shapes=[
            pltpu.VMEM(grads.shape, jnp.bfloat16),
            pltpu.VMEM(second_moment.shape, jnp.float32),
            pltpu.VMEM(arrived.shape, jnp.bfloat16),
            pltpu.VMEM(seeds.shape, jnp.bfloat16),
            pltpu.VMEM(fifth.shape, jnp.bfloat16),
            pltpu.VMEM(ratio.shape, jnp.float32),
            pltpu.VMEM(seeds.shape, jnp.bfloat16),
            pltpu.VMEM(returned_shape, jnp.bfloat16),
            pltpu.VMEM(second_moment.shape, jnp.float32),
            pltpu.SemaphoreType.DMA((4 * slots + 3,)),
            pltpu.SemaphoreType.DMA((slots + 3,)),
        ],
        compiler_params=grant(60),
        cost_estimate=cost(8 * slots, order, 24 * slots * order * order),
        name="owner",
    )(role, *square_halves, grads, second_moment, arrived, seeds, fifth, ratio)
    back = exchange(returned)

    placed, new_left, new_right = pl.pallas_call(
        functools.partial(finish_kernel, entries),
        out_shape=[
            jax.ShapeDtypeStruct((rows_dev, rows, width), jnp.bfloat16),
            jax.ShapeDtypeStruct(left_old.shape, jnp.float32),
            jax.ShapeDtypeStruct(right_old.shape, jnp.float32),
        ],
        in_specs=[SMEM, VMEM, VMEM, VMEM, VMEM, VMEM],
        out_specs=[VMEM, VMEM, VMEM],
        compiler_params=grant(16),
        name="finish",
    )(plan, *square_halves, left_old, right_old, back)
    return (placed, new_second, new_left[None], new_right[None], new_roots[None])


def solution(mesh):
    placed = (
        P("zero", "blk", None),
        P("zero", None, None),
        P("zero", None, "blk", None),
        P("zero", None, "blk", None),
        P("zero", "blk", None),
        P("zero", None, "blk", None, None),
    )
    return jax.shard_map(
        local,
        mesh=mesh,
        in_specs=placed,
        out_specs=(
            P("zero", "blk", None),
            P("zero", "blk", None),
            P("zero", None, "blk", None),
            P("zero", None, "blk", None),
            P("zero", None, "blk", None, None),
        ),
        check_vma=False,
    )
```

```python
import functools
import math

import jax
import jax.numpy as jnp
from jax import lax
from jax.experimental import pallas as pl
from jax.experimental.pallas import tpu as pltpu
from jax.sharding import PartitionSpec as P

BETA = 0.95
VMEM = pl.BlockSpec(memory_space=pltpu.VMEM)
SMEM = pl.BlockSpec(memory_space=pltpu.SMEM)
ANY = pl.BlockSpec(memory_space=pl.ANY)


def grant(mebibytes):
    return pltpu.CompilerParams(vmem_limit_bytes=mebibytes * 1024 * 1024)


def dot(former, latter):
    return jnp.dot(former, latter, preferred_element_type=jnp.float32)


def split(wide):
    high = wide.astype(jnp.bfloat16)
    return high, (wide - high.astype(jnp.float32)).astype(jnp.bfloat16)


LANES = 128
ROWS = 16
EXTRA = 8
HBM = pl.BlockSpec(memory_space=pltpu.HBM)


def thirds(wide):
    first = wide.astype(jnp.bfloat16).astype(jnp.float32)
    second = (wide - first).astype(jnp.bfloat16).astype(jnp.float32)
    return first, second, wide - first - second


def sublanes(shape):
    return lax.broadcasted_iota(jnp.int32, shape, len(shape) - 2)


def lanes(shape):
    return lax.broadcasted_iota(jnp.int32, shape, len(shape) - 1)


def span(tile):
    if isinstance(tile, int):
        return pl.ds(tile * ROWS, ROWS)
    return pl.ds(pl.multiple_of(tile * ROWS, ROWS), ROWS)


def store_piece(ref, place, first, piece):
    for tile in range(piece.shape[-1] // LANES):
        ref[place, span(first + tile)] = piece[:, tile * LANES : (tile + 1) * LANES]


def whole_block(ref, first, tiles):
    return jnp.concatenate(
        [ref[:, span(first + tile)].reshape(-1, LANES) for tile in range(tiles)], axis=1
    )


def scale_of(entries, half_ref, other_ref):
    total = half_ref[:1, :1] + other_ref[:1, :1]
    return jnp.minimum(1.0, math.sqrt(entries) / (jnp.sqrt(total) + 1e-06))


OWNER, HELPER, SPARE = 0, 1, 2


class Plan:
    def __init__(self, ref, blocks, devices):
        self.ref, self.blocks, self.devices = ref, blocks, devices

    @staticmethod
    def size(blocks, devices):
        return 3 * blocks + 3 * devices + 4

    def at(self, part, index):
        blocks, devices = self.blocks, self.devices
        start = {
            "slot": 0,
            "single": blocks,
            "owner": 2 * blocks,
            "load": 3 * blocks,
            "helper": 3 * blocks + devices,
            "idle": 3 * blocks + 2 * devices,
            "role": 3 * blocks + 3 * devices + 1,
            "own": 3 * blocks + 3 * devices + 2,
        }[part]
        return start + index

    def get(self, part, index=0):
        return self.ref[self.at(part, index)]

    def put(self, part, index, value):
        self.ref[self.at(part, index)] = value

    def share(self):
        return self.blocks // (self.devices - self.blocks)

    def spare_of(self, block):
        return self.get("idle", block // self.share())

    def fill(self, owner_ref, me):
        blocks, devices = self.blocks, self.devices
        spares = devices - blocks
        for device in range(devices):
            self.put("load", device, 0)
        for k in range(blocks):
            owner = owner_ref[k]
            slot = self.get("load", owner)
            self.put("owner", k, owner)
            self.put("slot", k, slot)
            self.put("load", owner, slot + 1)
        count, role = jnp.int32(0), jnp.int32(OWNER)
        for device in range(devices):
            idle = self.get("load", device) == 0
            self.put("idle", count, device)
            kind = jnp.where(count < spares, SPARE, HELPER)
            role = jnp.where(idle & (me == device), kind, role)
            count = count + idle.astype(jnp.int32)
        count = jnp.int32(spares)
        for device in range(devices):
            double = self.get("load", device) == 2
            helper = self.get("idle", jnp.minimum(count, devices - 1))
            self.put("helper", device, jnp.where(double, helper, device))
            count = count + double.astype(jnp.int32)
        self.put("role", 0, role)
        self.put("own", 0, self.get("load", me))


def pack_kernel(
    slots,
    me_ref,
    owner_ref,
    grads_hbm,
    left_hbm,
    right_hbm,
    out_hbm,
    plan_ref,
    role_ref,
    grads_ref,
    left_ref,
    right_ref,
    out_ref,
    in_sems,
    out_sems,
):
    rows_dev, rows, width = grads_ref.shape
    order = left_ref.shape[-1]
    cols = width // order
    blocks = rows_dev * cols
    tiles = order // LANES
    devices, extra = out_ref.shape[0], pl.ds(out_ref.shape[1] - EXTRA, EXTRA)
    parts = 4
    grads_in = pltpu.make_async_copy(grads_hbm, grads_ref, in_sems.at[0])
    grads_in.start()
    stats_in = []
    for part in range(parts):
        where = pl.ds(part * blocks // parts, blocks // parts)
        pair = []
        for side, (source, target) in enumerate(((left_hbm, left_ref), (right_hbm, right_ref))):
            pair.append(
                pltpu.make_async_copy(
                    source.at[where], target.at[where], in_sems.at[1 + 2 * part + side]
                )
            )
            pair[-1].start()
        stats_in.append(pair)
    me = me_ref[0]
    plan = Plan(plan_ref, blocks, devices)
    plan.fill(owner_ref, me)
    tile_row = sublanes((EXTRA, LANES))
    for owner in range(devices):
        out_ref[owner, extra] = jnp.zeros((EXTRA, LANES), jnp.bfloat16)
    grads_in.wait()
    for k in range(blocks):
        owner, slot = plan.get("owner", k), plan.get("slot", k)
        piece = grads_ref[k // cols, :, (k % cols) * order : (k % cols + 1) * order]
        store_piece(out_ref, owner, slot * tiles, piece)
        store_piece(out_ref, plan.get("helper", owner), slot * tiles, piece)
        store_piece(out_ref, plan.spare_of(k), k % plan.share() * tiles, piece)
    outs = []
    for turn, (first, count) in enumerate(
        (
            (0, slots * tiles * rows),
            (slots * tiles * rows, out_ref.shape[1] - slots * tiles * rows),
        )
    ):
        where = (slice(None), pl.ds(first, count))
        outs.append(
            pltpu.make_async_copy(out_ref.at[where], out_hbm.at[where], out_sems.at[turn])
        )
    outs[0].start()
    row = me * rows + sublanes((rows, order))
    lower = lanes((rows, order)) <= row
    mine = lanes((rows, order)) == row
    for k in range(blocks):
        if k % (blocks // parts) == 0:
            for copy in stats_in[k // (blocks // parts)]:
                copy.wait()
        owner, slot = plan.get("owner", k), plan.get("slot", k)
        right = right_ref[k]
        mixed = jnp.where(lower, left_ref[k], right).astype(jnp.bfloat16)
        store_piece(out_ref, owner, (slots + slot) * tiles, mixed)
        marked = jnp.where(mine, right, 0.0)
        diagonal = marked[:, :LANES]
        for tile in range(1, tiles):
            diagonal = diagonal + marked[:, tile * LANES : (tile + 1) * LANES]
        diagonal = jnp.sum(diagonal, axis=0, keepdims=True)
        out_ref[owner, extra] = jnp.where(
            tile_row == slot, diagonal, out_ref[owner, extra].astype(jnp.float32)
        ).astype(jnp.bfloat16)
    outs[1].start()
    role_ref[0] = plan.get("role")
    role_ref[1] = plan.get("own")
    own = [jnp.int32(0)] * slots
    for k in range(blocks):
        owner, slot = plan.get("owner", k), plan.get("slot", k)
        plan.put("single", k, (plan.get("load", owner) == 1).astype(jnp.int32))
        own = [jnp.where((owner == me) & (slot == i), k, own[i]) for i in range(slots)]
    for i in range(slots):
        role_ref[2 + i] = own[i]
    for copy in outs:
        copy.wait()


def square_kernel(grads_ref, _, __, out_ref):
    rows_dev, rows, width = grads_ref.shape
    total = jnp.zeros((8, 4 * LANES), jnp.float32)
    for i in range(rows_dev):
        for part in range(width // (4 * LANES)):
            wide = grads_ref[i, :, part * 4 * LANES : (part + 1) * 4 * LANES].astype(jnp.float32)
            wide = wide * wide
            for half in range(rows // 8):
                total = total + wide[8 * half : 8 * half + 8]
    out_ref[...] = jnp.broadcast_to(jnp.sum(total, keepdims=True), out_ref.shape)


def exact_ratio(diagonal):
    rounded = diagonal.astype(jnp.bfloat16).astype(jnp.float32)
    return jnp.where(rounded == 0.0, 1.0, diagonal / jnp.where(rounded == 0.0, 1.0, rounded))


def fifth_kernel(seed_ref, out_ref, ratio_ref):
    order = seed_ref.shape[-1]
    same = sublanes((order, order)) == lanes((order, order))
    for place in range(seed_ref.shape[0]):
        seed = seed_ref[place]
        high, low = split(dot(seed, seed))
        high, low = split(dot(high, high) + (dot(high, low) + dot(low, high)))
        fifth = -0.25 * (dot(seed, high) + dot(seed, low))
        marked = jnp.where(same, fifth, 0.0)
        across = exact_ratio(jnp.sum(marked, axis=0, keepdims=True))
        down = exact_ratio(jnp.sum(marked, axis=1, keepdims=True))
        out_ref[place] = (fifth / across).astype(jnp.bfloat16)
        ratio_ref[place] = jnp.broadcast_to(down, ratio_ref.shape[1:])


def adam_work(scale, grads_ref, second_ref, new_ref, order):
    rows_dev, rows, width = grads_ref.shape
    cols = width // order
    sums = jnp.zeros((1, LANES), jnp.float32)
    lane = lanes((1, LANES))
    for k in range(rows_dev * cols):
        where = (k // cols, slice(None), slice((k % cols) * order, (k % cols + 1) * order))
        clipped = grads_ref[where].astype(jnp.float32) * scale
        second = 0.95 * second_ref[where] + 0.05 * clipped * clipped
        new_ref[where] = second
        step = clipped / (jnp.sqrt(second) + 1e-08)
        sums = jnp.where(lane == k, jnp.sum(step * step, keepdims=True), sums)
    tile_row = sublanes((EXTRA, LANES))
    tile = jnp.zeros((EXTRA, LANES), jnp.float32)
    for place, term in enumerate(thirds(sums)):
        tile = jnp.where(tile_row == place, term, tile)
    return tile


def owner_kernel(
    slots,
    entries,
    role_ref,
    half_ref,
    other_ref,
    grads_hbm,
    second_hbm,
    arrived_hbm,
    seed_hbm,
    fifth_hbm,
    ratio_hbm,
    roots_hbm,
    out_hbm,
    new_hbm,
    grads_ref,
    second_ref,
    arrived_ref,
    seed_ref,
    fifth_ref,
    ratio_ref,
    roots_ref,
    out_ref,
    new_ref,
    in_sems,
    out_sems,
):
    devices, arrived_rows, lane_count = arrived_ref.shape
    order = seed_ref.shape[-1]
    tiles = order // lane_count
    piece = tiles * ROWS
    role, load = role_ref[0], role_ref[1]
    scale = scale_of(entries, half_ref, other_ref)
    factor = 0.05 * scale * scale

    sources = [(grads_hbm, grads_ref, ()), (second_hbm, second_ref, ())]
    sources.append((arrived_hbm, arrived_ref, (slice(None), pl.ds(0, piece))))
    mixed_at = (slice(None), pl.ds(slots * piece, arrived_rows - slots * piece))
    sources.append((arrived_hbm, arrived_ref, mixed_at))
    for slot in range(slots):
        if slot > 0:
            sources.append((arrived_hbm, arrived_ref, (slice(None), pl.ds(slot * piece, piece))))
        for source, target in ((fifth_hbm, fifth_ref), (ratio_hbm, ratio_ref), (seed_hbm, seed_ref)):
            sources.append((source, target, (slice(None), slot)))
    copies = [
        pltpu.make_async_copy(
            source.at[where] if where else source,
            target.at[where] if where else target,
            in_sems.at[place],
        )
        for place, (source, target, where) in enumerate(sources)
    ]
    for copy in copies:
        copy.start()
    adam_in, mixed_in = copies[:2], copies[3]
    gradient_in = [copies[2], copies[7]]
    root_in = [copies[4:7], copies[8:11]]
    shares = [
        (slice(None), pl.ds(0, piece)),
        (slice(None), pl.ds(piece, out_ref.shape[1] - piece)),
    ]
    outs = [
        pltpu.make_async_copy(out_ref.at[where], out_hbm.at[where], out_sems.at[place])
        for place, where in enumerate(shares)
    ] + [
        pltpu.make_async_copy(
            roots_ref.at[:, slot], roots_hbm.at[:, slot], out_sems.at[len(shares) + slot]
        )
        for slot in range(slots)
    ] + [pltpu.make_async_copy(new_ref, new_hbm, out_sems.at[len(shares) + slots])]
    for copy in adam_in:
        copy.wait()
    adam = adam_work(scale, grads_ref, second_ref, new_ref, order)
    outs[-1].start()

    def put_sums(norms):
        tile = adam
        tile_row, lane = sublanes((EXTRA, lane_count)), lanes((EXTRA, lane_count))
        for slot, norm in enumerate(norms):
            for place, term in enumerate(thirds(norm)):
                tile = jnp.where((tile_row == 3 + place) & (lane == role_ref[2 + slot]), term, tile)
        out_ref[:, pl.ds(out_ref.shape[1] - EXTRA, EXTRA)] = jnp.broadcast_to(
            tile.astype(jnp.bfloat16)[None], (devices, EXTRA, lane_count)
        )

    def put(first, value):
        value = value.astype(jnp.bfloat16)
        for tile in range(value.shape[1] // lane_count):
            out_ref[:, span(first + tile)] = value[
                :, tile * lane_count : (tile + 1) * lane_count
            ].reshape(devices, ROWS, lane_count)

    def gradient(slot):
        return whole_block(arrived_ref, slot * tiles, tiles)

    def right_gram(block):
        return lax.dot_general(
            block, block, (((0,), (0,)), ((), ())), preferred_element_type=jnp.float32
        )

    def left_part(block, start, stop):
        return lax.dot_general(
            block,
            block[start:stop],
            (((1,), (1,)), ((), ())),
            preferred_element_type=jnp.float32,
        )

    def old_stats(slot):
        mixed = whole_block(arrived_ref, (slots + slot) * tiles, tiles)
        turned = mixed.T.astype(jnp.float32)
        mixed = mixed.astype(jnp.float32)
        row, col = sublanes((order, order)), lanes((order, order))
        diagonal = []
        tile_row = sublanes((EXTRA, lane_count))
        for tile in range(tiles):
            total = jnp.zeros((EXTRA, lane_count), jnp.float32)
            for source in range(tile * devices // tiles, (tile + 1) * devices // tiles):
                total = total + arrived_ref[source, pl.ds(arrived_rows - EXTRA, EXTRA)].astype(
                    jnp.float32
                )
            diagonal.append(
                jnp.sum(jnp.where(tile_row == slot, total, 0.0), axis=0, keepdims=True)
            )
        diagonal = jnp.concatenate(diagonal, axis=1)
        left_old = jnp.where(col <= row, mixed, turned)
        right_old = jnp.where(col > row, mixed, jnp.where(col == row, diagonal, turned))
        return left_old, right_old

    def work(slot):
        gradient_in[slot].wait()
        block = gradient(slot)
        grams = left_part(block, 0, order), right_gram(block)
        if slot == 0:
            mixed_in.wait()
        olds = old_stats(slot)
        for copy in root_in[slot]:
            copy.wait()
        same = sublanes((order, order)) == lanes((order, order))
        new_pair = []
        for side, (old, gram) in enumerate(zip(olds, grams)):
            ratio = jnp.concatenate([ratio_ref[side, slot]] * tiles, axis=1)
            new = (BETA * old + factor * gram) * ratio
            across = exact_ratio(jnp.sum(jnp.where(same, new, 0.0), axis=0, keepdims=True))
            moved = dot(fifth_ref[side, slot], (new * (1.0 / across)).astype(jnp.bfloat16))
            root = 1.25 * seed_ref[side, slot].astype(jnp.float32) + moved * across
            new_pair.append(root.astype(jnp.bfloat16))
            roots_ref[side, slot] = new_pair[-1]
        outs[len(shares) + slot].start()
        applied = dot(new_pair[0], block).astype(jnp.bfloat16)
        direction = dot(applied, new_pair[1]).astype(jnp.bfloat16)
        put(slot * tiles, direction)
        wide = direction.astype(jnp.float32)
        norm = 1.0 / (jnp.sqrt(jnp.sum(wide * wide, keepdims=True)) + 1e-06)
        return grams, norm

    def keep(slot):
        for copy in root_in[slot]:
            copy.wait()
        for side in range(2):
            roots_ref[side, slot] = seed_ref[side, slot]
        outs[len(shares) + slot].start()

    @pl.when(load == 2)
    def _():
        (left, _), first = work(0)
        put(2 * tiles, left[:, :lane_count])
        outs[0].start()
        _, second = work(1)
        put_sums([first, second])
        outs[1].start()

    @pl.when(load == 1)
    def _():
        (left, right), first = work(0)
        outs[0].start()
        put(tiles, right)
        put(2 * tiles, left[:, :lane_count])
        put_sums([first])
        outs[1].start()
        gradient_in[1].wait()
        keep(1)

    @pl.when(load == 0)
    def _():
        gradient_in[0].wait()
        gradient_in[1].wait()
        mixed_in.wait()
        put_sums([])

        @pl.when(role == HELPER)
        def _():
            for slot in range(slots):
                put(slot * tiles, right_gram(gradient(slot)))
            put(slots * tiles, left_part(gradient(1), 0, lane_count))

        @pl.when(role == SPARE)
        def _():
            for turn in range(3):
                put(turn * (tiles - 1), left_part(gradient(turn), lane_count, order))

        outs[0].start()
        outs[1].start()
        keep(0)
        keep(1)

    for copy in outs:
        copy.wait()


def finish_kernel(
    entries,
    plan_ref,
    half_ref,
    other_ref,
    left_ref,
    right_ref,
    back_ref,
    out_ref,
    new_left_ref,
    new_right_ref,
):
    rows_dev, rows, width = out_ref.shape
    blocks, _, order = left_ref.shape
    cols = width // order
    tiles = order // LANES
    devices, extra = back_ref.shape[0], pl.ds(back_ref.shape[1] - EXTRA, EXTRA)
    plan = Plan(plan_ref, blocks, devices)
    factor = scale_of(entries, half_ref, other_ref)
    factor = 0.05 * factor * factor
    total = jnp.zeros((EXTRA, LANES), jnp.float32)
    for source in range(devices):
        total = total + back_ref[source, extra].astype(jnp.float32)
    tile_row, lane = sublanes((EXTRA, LANES)), lanes((EXTRA, LANES))
    norms = jnp.sqrt(jnp.sum(jnp.where(tile_row < 3, total, 0.0), axis=0, keepdims=True))
    inverse = (tile_row >= 3) & (tile_row < 6)
    norms = norms * jnp.sum(jnp.where(inverse, total, 0.0), axis=0, keepdims=True)
    for k in range(blocks):
        owner, slot = plan.get("owner", k), plan.get("slot", k)
        helper, single = plan.get("helper", owner), plan.get("single", k)
        spare = plan.spare_of(k)
        norm = jnp.sum(jnp.where(lane[:1] == k, norms, 0.0), axis=1, keepdims=True)
        right_from = jnp.where(single == 1, 1, slot) * tiles
        for tile in range(tiles):
            part = slice(tile * LANES, (tile + 1) * LANES)
            first = (k % cols) * order + tile * LANES
            out_ref[k // cols, :, first : first + LANES] = (
                back_ref[owner, span(slot * tiles + tile)].astype(jnp.float32) * norm
            ).astype(jnp.bfloat16)
            if tile == 0:
                gram = back_ref[jnp.where(slot == 0, owner, helper), span(2 * tiles)]
            else:
                gram = back_ref[spare, span(k % plan.share() * (tiles - 1) + tile - 1)]
            new_left_ref[k, :, part] = BETA * left_ref[k, :, part] + factor * gram.astype(
                jnp.float32
            )
            gram = back_ref[helper, span(right_from + tile)]
            new_right_ref[k, :, part] = BETA * right_ref[k, :, part] + factor * gram.astype(
                jnp.float32
            )


def swap(values, axis, bit):
    return lax.ppermute(values, axis, [(i, i ^ bit) for i in range(lax.axis_size(axis))])


def ring_sum(values, axis, unit):
    values = values + swap(values, axis, unit)
    return values + swap(values, axis, 3 * unit)


def blk_halves(values, axis, bit):
    size, width, near, halves = lax.axis_size("blk"), lax.axis_size("zero"), 4, 2
    values = ring_sum(values, "blk", 1)
    parts = []
    for turn in range(size // near // halves):
        pairs = []
        for place in range(size):
            for group in range(width):
                upper = ((place if axis == "blk" else group) // bit) % 2
                shift = near * (turn + upper * (size // near // halves))
                source = (place + shift) % size
                pairs.append((source * width + group, place * width + group))
        parts.append(lax.ppermute(values, ("blk", "zero"), pairs))
    half = functools.reduce(jnp.add, parts)
    return half, swap(half, axis, bit)


def exchange(values):
    return lax.all_to_all(values, "blk", split_axis=0, concat_axis=0, tiled=True)


def cost(passes, order, moved):
    return pl.CostEstimate(
        flops=2 * passes * order**3, bytes_accessed=moved, transcendentals=0
    )


def local(grads, owners, left_stats, right_stats, second_moment, roots):
    devices = lax.axis_size("blk")
    rows_dev, rows, width = grads.shape
    order = left_stats.shape[-1]
    cols = width // order
    blocks = rows_dev * cols
    slots = roots.shape[2]
    tiles = order // LANES
    entries = rows_dev * lax.axis_size("zero") * order * width
    me = lax.axis_index("blk").astype(jnp.int32).reshape(1)
    owner_of = owners.reshape(blocks)
    left_old, right_old, seeds = left_stats[0], right_stats[0], roots[0]

    sent_shape = (devices, 2 * slots * tiles * rows + EXTRA, LANES)
    sent, plan, role = pl.pallas_call(
        functools.partial(pack_kernel, slots),
        out_shape=[
            jax.ShapeDtypeStruct(sent_shape, jnp.bfloat16),
            jax.ShapeDtypeStruct((Plan.size(blocks, devices),), jnp.int32),
            jax.ShapeDtypeStruct((2 + slots,), jnp.int32),
        ],
        in_specs=[SMEM, SMEM, HBM, HBM, HBM],
        out_specs=[HBM, SMEM, SMEM],
        scratch_shapes=[
            pltpu.VMEM(grads.shape, jnp.bfloat16),
            pltpu.VMEM(left_old.shape, jnp.float32),
            pltpu.VMEM(right_old.shape, jnp.float32),
            pltpu.VMEM(sent_shape, jnp.bfloat16),
            pltpu.SemaphoreType.DMA((9,)),
            pltpu.SemaphoreType.DMA((2,)),
        ],
        compiler_params=grant(60),
        name="pack",
    )(me, owner_of, grads, left_old, right_old)
    arrived = exchange(sent)

    fifth, ratio = pl.pallas_call(
        fifth_kernel,
        out_shape=[
            jax.ShapeDtypeStruct((2 * slots, order, order), jnp.bfloat16),
            jax.ShapeDtypeStruct((2 * slots, order, LANES), jnp.float32),
        ],
        in_specs=[VMEM],
        out_specs=[VMEM, VMEM],
        compiler_params=grant(28),
        cost_estimate=cost(12 * slots, order, 12 * slots * order * order),
        name="fifth",
    )(seeds.reshape(2 * slots, order, order))
    square = pl.pallas_call(
        square_kernel,
        out_shape=jax.ShapeDtypeStruct((8, LANES), jnp.float32),
        in_specs=[VMEM, ANY, ANY],
        out_specs=VMEM,
        compiler_params=grant(8),
        name="square",
    )(grads, fifth, sent)
    square = ring_sum(square + swap(square, "zero", 1), "zero", 2)
    square_halves = blk_halves(square, "zero", 1)

    returned_shape = (devices, (2 * tiles + 1) * rows + EXTRA, LANES)
    fifth = fifth.reshape(2, slots, order, order)
    ratio = ratio.reshape(2, slots, order, LANES)
    new_roots, returned, new_second = pl.pallas_call(
        functools.partial(owner_kernel, slots, entries),
        out_shape=[
            jax.ShapeDtypeStruct(seeds.shape, jnp.bfloat16),
            jax.ShapeDtypeStruct(returned_shape, jnp.bfloat16),
            jax.ShapeDtypeStruct(second_moment.shape, jnp.float32),
        ],
        in_specs=[SMEM, VMEM, VMEM, HBM, HBM, HBM, HBM, HBM, HBM],
        out_specs=[HBM, HBM, HBM],
        scratch_shapes=[
            pltpu.VMEM(grads.shape, jnp.bfloat16),
            pltpu.VMEM(second_moment.shape, jnp.float32),
            pltpu.VMEM(arrived.shape, jnp.bfloat16),
            pltpu.VMEM(seeds.shape, jnp.bfloat16),
            pltpu.VMEM(fifth.shape, jnp.bfloat16),
            pltpu.VMEM(ratio.shape, jnp.float32),
            pltpu.VMEM(seeds.shape, jnp.bfloat16),
            pltpu.VMEM(returned_shape, jnp.bfloat16),
            pltpu.VMEM(second_moment.shape, jnp.float32),
            pltpu.SemaphoreType.DMA((4 * slots + 3,)),
            pltpu.SemaphoreType.DMA((slots + 3,)),
        ],
        compiler_params=grant(60),
        cost_estimate=cost(8 * slots, order, 24 * slots * order * order),
        name="owner",
    )(role, *square_halves, grads, second_moment, arrived, seeds, fifth, ratio)
    back = exchange(returned)

    placed, new_left, new_right = pl.pallas_call(
        functools.partial(finish_kernel, entries),
        out_shape=[
            jax.ShapeDtypeStruct((rows_dev, rows, width), jnp.bfloat16),
            jax.ShapeDtypeStruct(left_old.shape, jnp.float32),
            jax.ShapeDtypeStruct(right_old.shape, jnp.float32),
        ],
        in_specs=[SMEM, VMEM, VMEM, VMEM, VMEM, VMEM],
        out_specs=[VMEM, VMEM, VMEM],
        compiler_params=grant(16),
        name="finish",
    )(plan, *square_halves, left_old, right_old, back)
    return (placed, new_second, new_left[None], new_right[None], new_roots[None])


def solution(mesh):
    placed = (
        P("zero", "blk", None),
        P("zero", None, None),
        P("zero", None, "blk", None),
        P("zero", None, "blk", None),
        P("zero", "blk", None),
        P("zero", None, "blk", None, None),
    )
    return jax.shard_map(
        local,
        mesh=mesh,
        in_specs=placed,
        out_specs=(
            P("zero", "blk", None),
            P("zero", "blk", None),
            P("zero", None, "blk", None),
            P("zero", None, "blk", None),
            P("zero", None, "blk", None, None),
        ),
        check_vma=False,
    )
```
